128 devices in a mesh: dp: 32 (over y, z, core), noise: 4 (over x).
Axes of the slice: x: 4, y: 4, z: 4, core: 2. Of those that a mesh axis runs over, the one named last changes fastest.
Arguments:
- noise_latents: bfloat16 [1536, 16384], P('noise', 'dp'), may hold values from -6 to 6
- data_latents: bfloat16 [12288, 16384], P('dp'), may hold values from -6 to 6
Outputs:
- targets: bfloat16 [1536, 16384], P('noise', 'dp')
The draws below stay inside these ranges and needn't reach their ends.
All inputs are finite; a program needn't handle non-finite values.
Results may differ from the reference program's by a relative error of at most 0.022.
Values may be sent and summed in bfloat16 or wider, within the bound.
No kernel may reach another device: no remote copies, remote signals or barrier semaphores. Data moves between devices by JAX's collectives and lax.ppermute only.
A program may use at most 128 MiB of HBM per device.

```python
import jax
import jax.numpy as jnp

F = 16384
ITERS = 3
NN = 1536
ND = 12288


def shared_noise(key):
    return jnp.clip(jax.random.normal(key, (NN, F), jnp.float32), -6.0, 6.0)


def draw_noise_latents(key, part):
    base = shared_noise(key)
    return base.astype(jnp.bfloat16)


def draw_data_latents(key, part):
    key = jax.random.fold_in(key, 23)
    own = jnp.clip(jax.random.normal(key, (ND, F), jnp.float32), -6.0, 6.0)
    return own.astype(jnp.bfloat16)


def setup_inputs(seed: int = 0) -> dict:
    arg_keys = jax.random.split(jax.random.key(seed), 3)
    return {
        "noise_latents": draw_noise_latents(jax.random.fold_in(arg_keys[2], 71), 0),
        "data_latents": draw_data_latents(jax.random.fold_in(arg_keys[2], 71), 0),
    }


EPS = 0.004


def log_sum_exp(values, axis):
    peak = jnp.max(values, axis=axis, keepdims=True)
    total = jnp.sum(jnp.exp(values - peak), axis=axis)
    return jnp.squeeze(peak, axis) + jnp.log(total)


def reference(noise_latents, data_latents):
    dots = jnp.dot(noise_latents, data_latents.T, preferred_element_type=jnp.float32)
    noise_f = noise_latents.astype(jnp.float32)
    data_f = data_latents.astype(jnp.float32)
    sq_noise = jnp.sum(noise_f * noise_f, axis=1)
    sq_data = jnp.sum(data_f * data_f, axis=1)
    cost = (sq_noise[:, None] + sq_data[None, :] - 2.0 * dots) / F
    g_pot = jnp.zeros((data_latents.shape[0],), jnp.float32)
    for step in range(ITERS):
        f_pot = -EPS * log_sum_exp((g_pot[None, :] - cost) / EPS, 1)
        g_pot = -EPS * log_sum_exp((f_pot[:, None] - cost) / EPS, 0)
    scores = (g_pot[None, :] - cost) / EPS
    weights = jnp.exp(scores - log_sum_exp(scores, 1)[:, None]).astype(jnp.bfloat16)
    return jnp.dot(weights, data_latents, preferred_element_type=jnp.float32).astype(jnp.bfloat16)
```

```python
import jax
import jax.numpy as jnp
from jax import lax
from jax.sharding import PartitionSpec as P

ITERS = 3
EPS = 0.004


def lse(values, axis):
    peak = jnp.max(values, axis=axis, keepdims=True)
    total = jnp.sum(jnp.exp(values - peak), axis=axis)
    return jnp.squeeze(peak, axis) + jnp.log(total)


def to_all_dp(values):
    n = lax.axis_size("dp")
    return lax.all_to_all(
        jnp.broadcast_to(values[None], (n,) + values.shape), "dp", 0, 0
    )


def to_all_noise(values):
    n = lax.axis_size("noise")
    parts = [values]
    for k in range(1, n):
        parts.append(
            lax.ppermute(values, "noise", [(i, (i + k) % n) for i in range(n)])
        )
    return jnp.stack(parts)


def body(noise_latents, data_latents):
    width = data_latents.shape[1]
    piece = lax.all_gather(noise_latents, "dp", axis=1, tiled=True)
    dots = lax.dot_general(
        piece, data_latents, (((1,), (1,)), ((), ())), preferred_element_type=jnp.float32
    )
    noise_f = noise_latents.astype(jnp.float32)
    sx_part = jnp.sum(noise_f * noise_f, axis=1)
    data_f = data_latents.astype(jnp.float32)
    sq_data = jnp.sum(data_f * data_f, axis=1)
    scale = 1.0 / (width * EPS)
    twice = dots * (2.0 * scale)
    sy = sq_data * scale
    sx = None
    g = jnp.zeros_like(sy)
    for step in range(ITERS):
        local = lse(twice + (g - sy)[None, :], 1)
        if sx is None:
            got = to_all_dp(jnp.stack([local, sx_part]))
            sx = jnp.sum(got[:, 1], axis=0) * scale
            got = got[:, 0]
        else:
            got = to_all_dp(local)
        f = sx - lse(got, 0)
        local = lse(twice + (f - sx)[:, None], 0)
        g = sy - lse(to_all_noise(local), 0)
    coupling = jnp.exp(twice + (f - sx)[:, None] + (g - sy)[None, :])
    row_part = jnp.sum(coupling, axis=1)
    row_sum = jnp.sum(to_all_dp(row_part), axis=0)
    shares = lax.psum_scatter(
        lax.dot_general(
            data_latents,
            coupling.astype(jnp.bfloat16),
            (((0,), (1,)), ((), ())),
            preferred_element_type=jnp.float32,
        ).astype(jnp.bfloat16),
        "dp",
        scatter_dimension=0,
        tiled=True,
    ).astype(jnp.float32)
    return (shares.T / row_sum[:, None]).astype(jnp.bfloat16)


def solution(mesh):
    return jax.shard_map(
        body,
        mesh=mesh,
        in_specs=(P("noise", "dp"), P("dp", None)),
        out_specs=P("noise", "dp"),
        check_vma=False,
    )
```

```python
import jax
import jax.numpy as jnp
from jax import lax
from jax.experimental import pallas as pl
from jax.experimental.pallas import tpu as pltpu
from jax.sharding import PartitionSpec as P

ITERS = 3
EPS = 0.004
SIDE = 4
OFFS = (2, 1, 3)
VMEM = 48 * 1024 * 1024


def shift(values, dy, dz, dc=0):
    pairs = []
    for y in range(SIDE):
        for z in range(SIDE):
            for c in range(2):
                to = (((y + dy) % SIDE) * SIDE + (z + dz) % SIDE) * 2 + (c ^ dc)
                pairs.append(((y * SIDE + z) * 2 + c, to))
    return lax.ppermute(values, "dp", pairs)


def lse(values, axis):
    peak = jnp.max(values, axis=axis, keepdims=True)
    total = jnp.sum(jnp.exp(values - peak), axis=axis)
    return jnp.squeeze(peak, axis) + jnp.log(total)


def to_all_dp(values):
    n = lax.axis_size("dp")
    return lax.all_to_all(
        jnp.broadcast_to(values[None], (n,) + values.shape), "dp", 0, 0
    )


def to_all_noise(values):
    n = lax.axis_size("noise")
    parts = [values]
    for k in range(1, n):
        parts.append(
            lax.ppermute(values, "noise", [(i, (i + k) % n) for i in range(n)])
        )
    return jnp.stack(parts)


def other_columns(data, core):
    rows, width = data.shape
    block = width // (2 * SIDE * SIDE)

    def kernel(core_ref, in_ref, out_ref):
        out_ref[...] = in_ref[...]

    return pl.pallas_call(
        kernel,
        grid_spec=pltpu.PrefetchScalarGridSpec(
            num_scalar_prefetch=1,
            grid=(SIDE * SIDE,),
            in_specs=[pl.BlockSpec((rows, block), lambda t, c: (0, 2 * t + 1 - c[0]))],
            out_specs=pl.BlockSpec((rows, block), lambda t, c: (0, t)),
        ),
        out_shape=jax.ShapeDtypeStruct((rows, width // 2), data.dtype),
        compiler_params=pltpu.CompilerParams(vmem_limit_bytes=VMEM),
        cost_estimate=pl.CostEstimate(
            flops=0, bytes_accessed=rows * width * 2, transcendentals=0
        ),
    )(core, data)


def block_sum(w_own, w_oth, d_own, d_oth):
    total = jnp.dot(w_own[...], d_own[...], preferred_element_type=jnp.float32)
    total += jnp.dot(w_oth[...], d_oth[...], preferred_element_type=jnp.float32)
    return total.astype(jnp.bfloat16)


def sums(kernel, where, n, ins, out_shape, out_specs):
    w_own, w_oth, d_own, d_oth = ins
    rows, inner = w_own.shape
    block = d_own.shape[1] // (2 * SIDE * SIDE)
    return pl.pallas_call(
        kernel,
        grid_spec=pltpu.PrefetchScalarGridSpec(
            num_scalar_prefetch=1,
            grid=(n,),
            in_specs=[
                pl.BlockSpec((rows, inner), lambda t, w: (0, 0)),
                pl.BlockSpec((rows, inner), lambda t, w: (0, 0)),
                pl.BlockSpec((inner, block), lambda t, w: (0, 2 * w[t] + w[n])),
                pl.BlockSpec((inner, block), lambda t, w: (0, w[t])),
            ],
            out_specs=out_specs,
        ),
        out_shape=out_shape,
        compiler_params=pltpu.CompilerParams(vmem_limit_bytes=VMEM),
        cost_estimate=pl.CostEstimate(
            flops=n * 4 * rows * inner * block,
            bytes_accessed=n * (4 * inner * block + 2 * rows * block),
            transcendentals=0,
        ),
    )(where, *ins)


def far_kernel(where, w_own, w_oth, d_own, d_oth, *outs):
    t = pl.program_id(0)
    total = block_sum(w_own, w_oth, d_own, d_oth)
    half = total.shape[0] // 2
    for k in range(3):

        @pl.when(t // 3 == k)
        def _():
            outs[k][0] = total[:half]

        @pl.when(t % 3 == k)
        def _():
            outs[3 + k][0] = total[half:]


def near_kernel(where, w_own, w_oth, d_own, d_oth, along_z, along_y, mine):
    t = pl.program_id(0)
    total = block_sum(w_own, w_oth, d_own, d_oth)

    @pl.when(t < 3)
    def _():
        along_z[0] = total

    @pl.when((t >= 3) & (t < 6))
    def _():
        along_y[0] = total

    @pl.when(t == 6)
    def _():
        mine[...] = total


def scattered_sums(ins, y, z, core):
    rows = ins[0].shape[0]
    block = ins[2].shape[1] // (2 * SIDE * SIDE)
    half = rows // 2

    def places(offsets):
        chips = [((y + dy) % SIDE) * SIDE + (z + dz) % SIDE for dy, dz in offsets]
        return jnp.stack(chips + [core]).astype(jnp.int32)

    far = [(dy, dz) for dy in OFFS for dz in OFFS]
    part = jax.ShapeDtypeStruct((3, half, block), jnp.bfloat16)
    specs = []
    for k in range(3):
        specs.append(
            pl.BlockSpec(
                (1, half, block), lambda t, w, k=k: (jnp.clip(t - 3 * k, 0, 2), 0, 0)
            )
        )
    for k in range(3):
        specs.append(pl.BlockSpec((1, half, block), lambda t, w: (t // 3, 0, 0)))
    parts = sums(far_kernel, places(far), 9, ins, [part] * 6, specs)
    got_y = [shift(parts[k], OFFS[k], 0) for k in range(3)]
    got_z = [shift(parts[3 + k], 0, OFFS[k]) for k in range(3)]

    near = [(0, dz) for dz in OFFS] + [(dy, 0) for dy in OFFS] + [(0, 0)]
    whole = jax.ShapeDtypeStruct((3, rows, block), jnp.bfloat16)
    along_z, along_y, mine = sums(
        near_kernel,
        places(near),
        7,
        ins,
        [whole, whole, jax.ShapeDtypeStruct((rows, block), jnp.bfloat16)],
        [
            pl.BlockSpec((1, rows, block), lambda t, w: (jnp.minimum(t, 2), 0, 0)),
            pl.BlockSpec((1, rows, block), lambda t, w: (jnp.clip(t - 3, 0, 2), 0, 0)),
            pl.BlockSpec((rows, block), lambda t, w: (0, 0)),
        ],
    )

    def add(first, others):
        total = first.astype(jnp.float32)
        for other in others:
            total += other.astype(jnp.float32)
        return total

    sum_z = add(along_z[:, :half], got_y).astype(jnp.bfloat16)
    sum_y = add(along_y[:, half:], got_z).astype(jnp.bfloat16)
    got = []
    for k in range(3):
        got.append(shift(jnp.concatenate([sum_z[k], along_z[k, half:]]), 0, OFFS[k]))
        got.append(shift(jnp.concatenate([along_y[k, :half], sum_y[k]]), OFFS[k], 0))
    return add(mine, got)


def body(noise_latents, data_latents):
    width = data_latents.shape[1]
    place = lax.axis_index("dp")
    core = place % 2
    z = (place // 2) % SIDE
    y = place // (2 * SIDE)

    piece = lax.all_gather(noise_latents, "dp", axis=1, tiled=True)
    data_other = shift(other_columns(data_latents, core[None]), 0, 0, 1)
    dots = lax.dot_general(
        piece, data_latents, (((1,), (1,)), ((), ())), preferred_element_type=jnp.float32
    )
    noise_f = noise_latents.astype(jnp.float32)
    sx_part = jnp.sum(noise_f * noise_f, axis=1)
    data_f = data_latents.astype(jnp.float32)
    sq_data = jnp.sum(data_f * data_f, axis=1)
    scale = 1.0 / (width * EPS)
    twice = dots * (2.0 * scale)
    sy = sq_data * scale
    sx = None
    g = jnp.zeros_like(sy)
    for step in range(ITERS):
        local = lse(twice + (g - sy)[None, :], 1)
        if sx is None:
            got = to_all_dp(jnp.stack([local, sx_part]))
            sx = jnp.sum(got[:, 1], axis=0) * scale
            got = got[:, 0]
        else:
            got = to_all_dp(local)
        f = sx - lse(got, 0)
        local = lse(twice + (f - sx)[:, None], 0)
        g = sy - lse(to_all_noise(local), 0)
    coupling = jnp.exp(twice + (f - sx)[:, None] + (g - sy)[None, :])
    weights = coupling.astype(jnp.bfloat16)
    total = scattered_sums(
        (weights, shift(weights, 0, 0, 1), data_latents, data_other), y, z, core
    )
    row_sum = jnp.sum(to_all_dp(jnp.sum(coupling, axis=1)), axis=0)
    return (total / row_sum[:, None]).astype(jnp.bfloat16)


def solution(mesh):
    return jax.shard_map(
        body,
        mesh=mesh,
        in_specs=(P("noise", "dp"), P("dp", None)),
        out_specs=P("noise", "dp"),
        check_vma=False,
    )
```

```python
import jax
import jax.numpy as jnp
from jax import lax
from jax.experimental import pallas as pl
from jax.experimental.pallas import tpu as pltpu
from jax.sharding import PartitionSpec as P

ITERS = 3
EPS = 0.004
SIDE = 4
OFFS = (2, 1, 3)
BLOCKS = SIDE * SIDE
VMEM = 48 * 1024 * 1024


def swap(values):
    n = lax.axis_size("dp")
    return lax.ppermute(values, "dp", [(i, i ^ 1) for i in range(n)])


def hop(values, k, first):
    pairs = []
    for y in range(SIDE):
        for z in range(SIDE):
            for c in range(2):
                along_z = (c == 0) == first
                to_y, to_z = (y, (z + k) % SIDE) if along_z else ((y + k) % SIDE, z)
                pairs.append(((y * SIDE + z) * 2 + c, (to_y * SIDE + to_z) * 2 + c))
    return lax.ppermute(values, "dp", pairs)


def block_ids(y, z, core):
    spots = [(0, 0, 0)]
    spots += [(0, m, b) for m in OFFS for b in (0, 1)]
    spots += [(k, m, 0) for k in OFFS for m in OFFS]
    ids = []
    for k, m, b in spots:
        dy = jnp.where(core == 0, k, m)
        dz = jnp.where(core == 0, m, k)
        chip = ((y + dy) % SIDE) * SIDE + (z + dz) % SIDE
        ids.append(chip * 2 + jnp.where(core == 0, b, 1 - b))
    return jnp.stack(ids).astype(jnp.int32)


def lse(values, axis):
    peak = jnp.max(values, axis=axis, keepdims=True)
    total = jnp.sum(jnp.exp(values - peak), axis=axis)
    return jnp.squeeze(peak, axis) + jnp.log(total)


def to_all_dp(values):
    n = lax.axis_size("dp")
    return lax.all_to_all(
        jnp.broadcast_to(values[None], (n,) + values.shape), "dp", 0, 0
    )


def to_all_noise(values):
    n = lax.axis_size("noise")
    parts = [values]
    for k in range(1, n):
        parts.append(
            lax.ppermute(values, "noise", [(i, (i + k) % n) for i in range(n)])
        )
    return jnp.stack(parts)


def call(kernel, ids, ins, out_shape, scratch, flops, moved):
    return pl.pallas_call(
        kernel,
        in_specs=[pl.BlockSpec(memory_space=pltpu.SMEM)]
        + [pl.BlockSpec(memory_space=pl.ANY)] * len(ins),
        out_specs=[pl.BlockSpec(memory_space=pl.ANY)] * len(out_shape),
        out_shape=out_shape,
        scratch_shapes=scratch,
        compiler_params=pltpu.CompilerParams(vmem_limit_bytes=VMEM),
        cost_estimate=pl.CostEstimate(
            flops=flops, bytes_accessed=moved, transcendentals=0
        ),
    )(ids, *ins)


def columns(ref, place, block):
    return ref.at[:, pl.ds(pl.multiple_of(place * block, block), block)]


def picked_columns(data, ids):
    rows, width = data.shape
    block = width // (2 * BLOCKS)

    def kernel(ids_ref, in_ref, out_ref, sems):
        copies = []
        for t in range(BLOCKS):
            copies.append(
                pltpu.make_async_copy(
                    columns(in_ref, ids_ref[t], block),
                    out_ref.at[:, pl.ds(t * block, block)],
                    sems.at[t],
                )
            )
            copies[-1].start()
        for copy in copies:
            copy.wait()

    return call(
        kernel,
        ids,
        [data],
        [jax.ShapeDtypeStruct((rows, width // 2), data.dtype)],
        [pltpu.SemaphoreType.DMA((BLOCKS,))],
        0,
        rows * width * 2,
    )[0]


def part_dots(ids, start, groups, data, data_other, before):
    sizes = [g.shape[0] for g in groups]
    n = sum(sizes)
    rows, block = groups[0].shape[1:]
    inner = data.shape[0]
    spots = [(a, i) for a, size in enumerate(sizes) for i in range(size)]
    n_in = len(groups) + 2 + (0 if before is None else 2)

    def kernel(ids_ref, *refs):
        ins, (own, oth) = refs[:n_in], refs[n_in : n_in + 2]
        pieces, d_own, d_oth, acc, sems, acc_sems = refs[n_in + 2 :]
        data_ref, data_other_ref = ins[len(groups) : len(groups) + 2]
        copies = []
        if before is not None:
            for b in range(2):
                copy = pltpu.make_async_copy(
                    ins[len(groups) + 2 + b], acc.at[b], acc_sems.at[b]
                )
                copy.start()
                copies.append(copy)
        steps = []
        for t, (a, i) in enumerate(spots):
            sources = (
                ins[a].at[i],
                columns(data_ref, ids_ref[t + start], block),
                data_other_ref.at[:, pl.ds((t + start) * block, block)],
            )
            steps.append(
                [
                    pltpu.make_async_copy(source, to.at[t], sems.at[b, t])
                    for b, (source, to) in enumerate(
                        zip(sources, (pieces, d_own, d_oth))
                    )
                ]
            )
            for copy in steps[-1]:
                copy.start()
        for copy in copies:
            copy.wait()
        for t, step in enumerate(steps):
            for copy in step:
                copy.wait()
            for b, d in enumerate((d_own, d_oth)):
                part = lax.dot_general(
                    pieces[t],
                    d[t],
                    (((1,), (1,)), ((), ())),
                    preferred_element_type=jnp.float32,
                )
                if t == 0 and before is None:
                    acc[b] = part
                else:
                    acc[b] += part
        copies = []
        for b, out in enumerate((own, oth)):
            copies.append(pltpu.make_async_copy(acc.at[b], out, acc_sems.at[b]))
            copies[-1].start()
        for copy in copies:
            copy.wait()

    shape = jax.ShapeDtypeStruct((rows, inner), jnp.float32)
    return call(
        kernel,
        ids,
        list(groups) + [data, data_other] + ([] if before is None else list(before)),
        [shape, shape],
        [
            pltpu.VMEM((n, rows, block), data.dtype),
            pltpu.VMEM((n, inner, block), data.dtype),
            pltpu.VMEM((n, inner, block), data.dtype),
            pltpu.VMEM((2, rows, inner), jnp.float32),
            pltpu.SemaphoreType.DMA((3, n)),
            pltpu.SemaphoreType.DMA((2,)),
        ],
        n * 4 * rows * inner * block,
        n * block * (4 * inner + 2 * rows),
    )


def gathered_dots(noise, data, data_other, ids):
    both = jnp.stack([noise, swap(noise)])
    first = [hop(both, -k, True) for k in OFFS]
    passing = jnp.stack([got[0] for got in first])
    second = [hop(passing, -k, False) for k in OFFS]
    dots = part_dots(ids, 0, [noise[None]] + first, data, data_other, None)
    own, other = part_dots(ids, 7, second, data, data_other, dots)
    return own + swap(other)


def part_sums(ids, start, sizes, ins):
    rows, inner = ins[0].shape
    dtype = ins[2].dtype
    block = ins[3].shape[1] // BLOCKS
    spots = [(a, i) for a, size in enumerate(sizes) for i in range(size)]
    n = len(spots)

    def kernel(ids_ref, w_own_ref, w_oth_ref, data_ref, data_other_ref, *refs):
        outs = refs[: len(sizes)]
        weights, d_own, d_oth, totals, w_sems, sems = refs[len(sizes) :]
        first = []
        for b, w in enumerate((w_own_ref, w_oth_ref)):
            first.append(pltpu.make_async_copy(w, weights.at[b], w_sems.at[b]))
            first[-1].start()
        steps = []
        for t in range(n):
            sources = (
                columns(data_ref, ids_ref[t + start], block),
                data_other_ref.at[:, pl.ds((t + start) * block, block)],
            )
            steps.append(
                [
                    pltpu.make_async_copy(source, to.at[t], sems.at[b, t])
                    for b, (source, to) in enumerate(zip(sources, (d_own, d_oth)))
                ]
            )
            for copy in steps[-1]:
                copy.start()
        for copy in first:
            copy.wait()
        last = []
        for t, (a, i) in enumerate(spots):
            for copy in steps[t]:
                copy.wait()
            total = jnp.dot(weights[0], d_own[t], preferred_element_type=jnp.float32)
            total += jnp.dot(weights[1], d_oth[t], preferred_element_type=jnp.float32)
            totals[t] = total.astype(dtype)
            last.append(pltpu.make_async_copy(totals.at[t], outs[a].at[i], sems.at[2, t]))
            last[-1].start()
        for copy in last:
            copy.wait()

    return call(
        kernel,
        ids,
        ins,
        [jax.ShapeDtypeStruct((size, rows, block), dtype) for size in sizes],
        [
            pltpu.VMEM((2, rows, inner), dtype),
            pltpu.VMEM((n, inner, block), dtype),
            pltpu.VMEM((n, inner, block), dtype),
            pltpu.VMEM((n, rows, block), dtype),
            pltpu.SemaphoreType.DMA((2,)),
            pltpu.SemaphoreType.DMA((3, n)),
        ],
        n * 4 * rows * inner * block,
        n * (4 * inner * block + 2 * rows * block),
    )


def added(first, others):
    total = first.astype(jnp.float32)
    for other in others:
        total += other.astype(jnp.float32)
    return total


def scattered_sums(ids, ins, row_part):
    far = part_sums(ids, 7, [3, 3, 3], ins)
    got = [hop(part, k, False) for part, k in zip(far, OFFS)]
    mine, *near = part_sums(ids, 0, [1, 2, 2, 2], ins)
    row_part, *near = lax.optimization_barrier((row_part, *near))
    row_sum = jnp.sum(to_all_dp(row_part), axis=0)
    row_sum, *got = lax.optimization_barrier((row_sum, *got))
    last = []
    for a, k in enumerate(OFFS):
        total = added(near[a][0], [g[a] for g in got]).astype(jnp.bfloat16)
        last.append(hop(jnp.stack([total, near[a][1]]), k, True))
    other = added(last[0][1], [g[1] for g in last[1:]])
    return added(mine[0], [g[0] for g in last] + [swap(other)]), row_sum


def body(noise_latents, data_latents):
    width = data_latents.shape[1]
    place = lax.axis_index("dp")
    core = place % 2
    z = (place // 2) % SIDE
    y = place // (2 * SIDE)
    ids = block_ids(y, z, core)
    data_other = swap(picked_columns(data_latents, block_ids(y, z, 1 - core)))
    dots = gathered_dots(noise_latents, data_latents, data_other, ids)
    noise_f = noise_latents.astype(jnp.float32)
    sx_part = jnp.sum(noise_f * noise_f, axis=1)
    data_f = data_latents.astype(jnp.float32)
    sq_data = jnp.sum(data_f * data_f, axis=1)
    scale = 1.0 / (width * EPS)
    twice = dots * (2.0 * scale)
    sy = sq_data * scale
    sx = None
    g = jnp.zeros_like(sy)
    for step in range(ITERS):
        local = lse(twice + (g - sy)[None, :], 1)
        if sx is None:
            got = to_all_dp(jnp.stack([local, sx_part]))
            sx = jnp.sum(got[:, 1], axis=0) * scale
            got = got[:, 0]
        else:
            got = to_all_dp(local)
        f = sx - lse(got, 0)
        local = lse(twice + (f - sx)[:, None], 0)
        g = sy - lse(to_all_noise(local), 0)
    coupling = jnp.exp(twice + (f - sx)[:, None] + (g - sy)[None, :])
    weights = coupling.astype(jnp.bfloat16)
    total, row_sum = scattered_sums(
        ids,
        (weights, swap(weights), data_latents, data_other),
        jnp.sum(coupling, axis=1),
    )
    return (total / row_sum[:, None]).astype(jnp.bfloat16)


def solution(mesh):
    return jax.shard_map(
        body,
        mesh=mesh,
        in_specs=(P("noise", "dp"), P("dp", None)),
        out_specs=P("noise", "dp"),
        check_vma=False,
    )
```

```python
import jax
import jax.numpy as jnp
from jax import lax
from jax.experimental import pallas as pl
from jax.experimental.pallas import tpu as pltpu
from jax.sharding import PartitionSpec as P

ITERS = 3
EPS = 0.004
SIDE = 4
OFFS = (2, 1, 3)
BLOCKS = SIDE * SIDE
VMEM = 48 * 1024 * 1024

SPOTS = [(k, m) for k in (0, 1, 3, 2) for m in OFFS + (0,)]


def swap(values):
    n = lax.axis_size("dp")
    return lax.ppermute(values, "dp", [(i, i ^ 1) for i in range(n)])


def hop(values, k, first):
    pairs = []
    for y in range(SIDE):
        for z in range(SIDE):
            for c in range(2):
                along_z = (c == 0) == first
                to_y, to_z = (y, (z + k) % SIDE) if along_z else ((y + k) % SIDE, z)
                pairs.append(((y * SIDE + z) * 2 + c, (to_y * SIDE + to_z) * 2 + c))
    return lax.ppermute(values, "dp", pairs)


def block_ids(y, z, core):
    ids = []
    for k, m in SPOTS:
        dy = jnp.where(core == 0, k, m)
        dz = jnp.where(core == 0, m, k)
        ids.append((((y + dy) % SIDE) * SIDE + (z + dz) % SIDE) * 2 + core)
    return jnp.stack(ids).astype(jnp.int32)


def lse(values, axis):
    peak = jnp.max(values, axis=axis, keepdims=True)
    total = jnp.sum(jnp.exp(values - peak), axis=axis)
    return jnp.squeeze(peak, axis) + jnp.log(total)


def to_all_dp(values):
    n = lax.axis_size("dp")
    return lax.all_to_all(
        jnp.broadcast_to(values[None], (n,) + values.shape), "dp", 0, 0
    )


def to_all_noise(values):
    n = lax.axis_size("noise")
    parts = [values]
    for k in range(1, n):
        parts.append(
            lax.ppermute(values, "noise", [(i, (i + k) % n) for i in range(n)])
        )
    return jnp.stack(parts)


def call(kernel, ids, ins, out_shape, scratch, flops, moved):
    return pl.pallas_call(
        kernel,
        in_specs=[pl.BlockSpec(memory_space=pltpu.SMEM)]
        + [pl.BlockSpec(memory_space=pl.ANY)] * len(ins),
        out_specs=[pl.BlockSpec(memory_space=pl.ANY)] * len(out_shape),
        out_shape=out_shape,
        scratch_shapes=scratch,
        compiler_params=pltpu.CompilerParams(vmem_limit_bytes=VMEM),
        cost_estimate=pl.CostEstimate(
            flops=flops, bytes_accessed=moved, transcendentals=0
        ),
    )(ids, *ins)


def columns(ref, place, block):
    return ref.at[:, pl.ds(pl.multiple_of(place * block, block), block)]


def part_dots(ids, start, groups, data, data_other, before):
    sizes = [g[0].shape[0] for g in groups]
    n = sum(sizes)
    rows = sum(p.shape[1] for p in groups[0])
    block = groups[0][0].shape[2]
    inner = data.shape[0]
    spots = [(a, i) for a, size in enumerate(sizes) for i in range(size)]
    parts = [p for g in groups for p in g]
    per = len(groups[0])
    height = rows // per
    n_in = len(parts) + 2 + (0 if before is None else 2)

    def kernel(ids_ref, *refs):
        ins, outs = refs[:n_in], refs[n_in : n_in + 2]
        pieces, held, acc, sems, acc_sems = refs[n_in + 2 :]
        data_ref, data_other_ref = ins[len(parts) : len(parts) + 2]
        halves = [acc.at[:, pl.ds(b * inner, inner)] for b in range(2)]
        first = []
        if before is not None:
            for b in range(2):
                source = ins[len(parts) + 2 + b]
                first.append(
                    pltpu.make_async_copy(source, halves[b], acc_sems.at[b])
                )
                first[-1].start()
        steps = []
        for t, (a, i) in enumerate(spots):
            places = [
                (ins[a * per + p].at[i], pieces.at[t, pl.ds(p * height, height)])
                for p in range(per)
            ] + [
                (
                    columns(data_ref, ids_ref[t + start], block),
                    held.at[t, pl.ds(0, inner)],
                ),
                (
                    columns(data_other_ref, ids_ref[t + start], block),
                    held.at[t, pl.ds(inner, inner)],
                ),
            ]
            steps.append(
                [
                    pltpu.make_async_copy(source, to, sems.at[b, t])
                    for b, (source, to) in enumerate(places)
                ]
            )
            for copy in steps[-1]:
                copy.start()
        for copy in first:
            copy.wait()
        for t, step in enumerate(steps):
            for copy in step:
                copy.wait()
            part = lax.dot_general(
                pieces[t],
                held[t],
                (((1,), (1,)), ((), ())),
                preferred_element_type=jnp.float32,
            )
            if t == 0 and before is None:
                acc[...] = part
            else:
                acc[...] += part
        last = []
        for b in range(2):
            last.append(pltpu.make_async_copy(halves[b], outs[b], acc_sems.at[b]))
            last[-1].start()
        for copy in last:
            copy.wait()

    shape = jax.ShapeDtypeStruct((rows, inner), jnp.float32)
    return call(
        kernel,
        ids,
        parts + [data, data_other] + ([] if before is None else list(before)),
        [shape, shape],
        [
            pltpu.VMEM((n, rows, block), data.dtype),
            pltpu.VMEM((n, 2 * inner, block), data.dtype),
            pltpu.VMEM((rows, 2 * inner), jnp.float32),
            pltpu.SemaphoreType.DMA((per + 2, n)),
            pltpu.SemaphoreType.DMA((2,)),
        ],
        n * 4 * rows * inner * block,
        n * block * (4 * inner + 2 * rows),
    )


def gathered_dots(noise, data, data_other, ids, sq_data):
    half = noise.shape[0] // 2
    along = [hop(noise, -k, True) for k in OFFS] + [noise]
    top = jnp.stack([block[:half] for block in along])
    bottom = jnp.stack([block[half:] for block in along])
    top, bottom, sq_data = lax.optimization_barrier((top, bottom, sq_data))
    up_top, down_bottom = hop(top, -1, False), hop(bottom, 1, False)
    up_bottom, down_top = hop(bottom, -1, False), hop(top, 1, False)
    groups = [[block[None]] for block in along]
    dots = part_dots(ids, 0, groups, data, data_other, None)
    up_top, down_bottom, *dots = lax.optimization_barrier((up_top, down_bottom, *dots))
    far = [hop(up_top, -1, False), hop(down_bottom, 1, False)]
    groups = [[up_top, up_bottom], [down_top, down_bottom]]
    dots = part_dots(ids, 4, groups, data, data_other, dots)
    own, other = part_dots(ids, 12, [far], data, data_other, dots)
    return own + swap(other), sq_data


def part_sums(ids, start, sizes, ins, per=1):
    rows, inner = ins[0].shape
    dtype = ins[2].dtype
    block = ins[2].shape[1] // (2 * BLOCKS)
    spots = [(a, i) for a, size in enumerate(sizes) for i in range(size)]
    n = len(spots)
    height = rows // per

    def kernel(ids_ref, w_own_ref, w_oth_ref, data_ref, data_other_ref, *refs):
        outs = refs[: per * len(sizes)]
        weights, held, totals, w_sems, sems = refs[per * len(sizes) :]
        first = []
        for b, w in enumerate((w_own_ref, w_oth_ref)):
            to = weights.at[:, pl.ds(b * inner, inner)]
            first.append(pltpu.make_async_copy(w, to, w_sems.at[b]))
            first[-1].start()
        steps = []
        for t in range(n):
            sources = [
                columns(ref, ids_ref[t + start], block)
                for ref in (data_ref, data_other_ref)
            ]
            steps.append(
                [
                    pltpu.make_async_copy(
                        source, held.at[t, pl.ds(b * inner, inner)], sems.at[b, t]
                    )
                    for b, source in enumerate(sources)
                ]
            )
            for copy in steps[-1]:
                copy.start()
        for copy in first:
            copy.wait()
        last = []
        for t, (a, i) in enumerate(spots):
            for copy in steps[t]:
                copy.wait()
            total = jnp.dot(weights[...], held[t], preferred_element_type=jnp.float32)
            totals[t] = total.astype(dtype)
            for p in range(per):
                source = totals.at[t, pl.ds(p * height, height)]
                to = outs[a * per + p].at[i]
                last.append(pltpu.make_async_copy(source, to, sems.at[2 + p, t]))
                last[-1].start()
        for copy in last:
            copy.wait()

    return call(
        kernel,
        ids,
        ins,
        [
            jax.ShapeDtypeStruct((size, height, block), dtype)
            for size in sizes
            for p in range(per)
        ],
        [
            pltpu.VMEM((rows, 2 * inner), dtype),
            pltpu.VMEM((n, 2 * inner, block), dtype),
            pltpu.VMEM((n, rows, block), dtype),
            pltpu.SemaphoreType.DMA((2,)),
            pltpu.SemaphoreType.DMA((2 + per, n)),
        ],
        n * 4 * rows * inner * block,
        n * (4 * inner * block + 2 * rows * block),
    )


def added(first, others):
    total = first.astype(jnp.float32)
    for other in others:
        total += other.astype(jnp.float32)
    return total


def scattered_sums(ids, ins, row_part):
    top, bottom = part_sums(ids, 12, [4], ins, 2)
    ids, top, bottom = lax.optimization_barrier((ids, top, bottom))
    top, bottom = hop(top, 1, False), hop(bottom, -1, False)
    up_top, up_bottom, down_top, down_bottom = part_sums(ids, 4, [4, 4], ins, 2)
    ids, up_bottom, down_top = lax.optimization_barrier((ids, up_bottom, down_top))
    tops, bottoms = [hop(down_top, -1, False)], [hop(up_bottom, 1, False)]
    near_top, near_bottom = part_sums(ids, 0, [4], ins, 2)
    tops.append(hop(added(up_top, [top]).astype(top.dtype), 1, False))
    bottoms.append(hop(added(down_bottom, [bottom]).astype(top.dtype), -1, False))
    totals = []
    for a in range(3):
        total = [
            added(near_top[a], [got[a] for got in tops]),
            added(near_bottom[a], [got[a] for got in bottoms]),
        ]
        totals.append(jnp.concatenate(total).astype(top.dtype))
    row_part, *totals = lax.optimization_barrier((row_part, *totals))
    sums = [hop(total, k, True) for total, k in zip(totals, OFFS)]
    row_sum = jnp.sum(to_all_dp(row_part), axis=0)
    row_sum, near_top = lax.optimization_barrier((row_sum, near_top))
    total = [
        added(near_top[3], [got[3] for got in tops]),
        added(near_bottom[3], [got[3] for got in bottoms]),
    ]
    return added(jnp.concatenate(total), sums), row_sum


def body(noise_latents, data_latents):
    width = data_latents.shape[1]
    place = lax.axis_index("dp")
    core = place % 2
    z = (place // 2) % SIDE
    y = place // (2 * SIDE)
    ids = block_ids(y, z, core)
    data_other = swap(data_latents)
    noise_f = noise_latents.astype(jnp.float32)
    sx_part = jnp.sum(noise_f * noise_f, axis=1)
    data_f = data_latents.astype(jnp.float32)
    sq_data = jnp.sum(data_f * data_f, axis=1)
    dots, sq_data = gathered_dots(
        noise_latents, data_latents, data_other, ids, sq_data
    )
    scale = 1.0 / (width * EPS)
    twice = dots * (2.0 * scale)
    sy = sq_data * scale
    sx = None
    g = jnp.zeros_like(sy)
    for step in range(ITERS):
        local = lse(twice + (g - sy)[None, :], 1)
        if sx is None:
            got = to_all_dp(jnp.stack([local, sx_part]))
            sx = jnp.sum(got[:, 1], axis=0) * scale
            got = got[:, 0]
        else:
            got = to_all_dp(local)
        f = sx - lse(got, 0)
        local = lse(twice + (f - sx)[:, None], 0)
        g = sy - lse(to_all_noise(local), 0)
    coupling = jnp.exp(twice + (f - sx)[:, None] + (g - sy)[None, :])
    weights = coupling.astype(jnp.bfloat16)
    total, row_sum = scattered_sums(
        ids,
        (weights, swap(weights), data_latents, data_other),
        jnp.sum(coupling, axis=1),
    )
    return (total / row_sum[:, None]).astype(jnp.bfloat16)


def solution(mesh):
    return jax.shard_map(
        body,
        mesh=mesh,
        in_specs=(P("noise", "dp"), P("dp", None)),
        out_specs=P("noise", "dp"),
        check_vma=False,
    )
```

```python
import jax
import jax.numpy as jnp
from jax import lax
from jax.experimental import pallas as pl
from jax.experimental.pallas import tpu as pltpu
from jax.sharding import PartitionSpec as P

ITERS = 3
EPS = 0.004
SIDE = 4
OFFS = (2, 1, 3)
BLOCKS = SIDE * SIDE
VMEM_LIMIT = 24 * 1024 * 1024

SPOTS = [(k, m) for k in (0, 1, 3, 2) for m in OFFS + (0,)]


def swap(values):
    n = lax.axis_size("dp")
    return lax.ppermute(values, "dp", [(i, i ^ 1) for i in range(n)])


def hop(values, k, first):
    pairs = []
    for y in range(SIDE):
        for z in range(SIDE):
            for c in range(2):
                along_z = (c == 0) == first
                to_y, to_z = (y, (z + k) % SIDE) if along_z else ((y + k) % SIDE, z)
                pairs.append(((y * SIDE + z) * 2 + c, (to_y * SIDE + to_z) * 2 + c))
    return lax.ppermute(values, "dp", pairs)


def block_ids(y, z, core):
    ids = []
    for k, m in SPOTS:
        dy = jnp.where(core == 0, k, m)
        dz = jnp.where(core == 0, m, k)
        ids.append((((y + dy) % SIDE) * SIDE + (z + dz) % SIDE) * 2 + core)
    return jnp.stack(ids).astype(jnp.int32)


def lse(values, axis):
    peak = jnp.max(values, axis=axis, keepdims=True)
    total = jnp.sum(jnp.exp(values - peak), axis=axis)
    return jnp.squeeze(peak, axis) + jnp.log(total)


def to_all_dp(values):
    n = lax.axis_size("dp")
    return lax.all_to_all(
        jnp.broadcast_to(values[None], (n,) + values.shape), "dp", 0, 0
    )


def to_all_noise(values):
    n = lax.axis_size("noise")
    parts = [values]
    for k in range(1, n):
        parts.append(
            lax.ppermute(values, "noise", [(i, (i + k) % n) for i in range(n)])
        )
    return jnp.stack(parts)


def call(kernel, ins, in_specs, out_shape, out_specs, scratch, flops, moved):
    return pl.pallas_call(
        kernel,
        in_specs=in_specs,
        out_specs=out_specs,
        out_shape=out_shape,
        scratch_shapes=scratch,
        compiler_params=pltpu.CompilerParams(vmem_limit_bytes=VMEM_LIMIT),
        cost_estimate=pl.CostEstimate(
            flops=flops, bytes_accessed=moved, transcendentals=0
        ),
    )(*ins)


IN_SMEM = pl.BlockSpec(memory_space=pltpu.SMEM)
IN_VMEM = pl.BlockSpec(memory_space=pltpu.VMEM)
ANYWHERE = pl.BlockSpec(memory_space=pl.ANY)


def in_hbm(arrays):
    return [pltpu.with_memory_space_constraint(a, pltpu.HBM) for a in arrays]


def block_copies(ids_ref, t, refs, to, spot, sems):
    rows, width = refs[0].shape
    block = width // (2 * BLOCKS)
    place = pl.multiple_of(ids_ref[t] * block, block)
    return [
        pltpu.make_async_copy(
            ref.at[:, pl.ds(place, block)],
            to.at[pl.ds(b * rows, rows), pl.ds(spot * block, block)],
            sems.at[b, spot],
        )
        for b, ref in enumerate(refs)
    ]


def held_blocks(ids, data, data_other):
    rows, width = data.shape

    def kernel(ids_ref, data_ref, data_other_ref, held, sems):
        copies = []
        for t in range(BLOCKS):
            copies += block_copies(
                ids_ref, t, (data_ref, data_other_ref), held, t, sems
            )
        for copy in copies:
            copy.start()
        for copy in copies:
            copy.wait()

    return call(
        kernel,
        [ids] + in_hbm([data, data_other]),
        [IN_SMEM, ANYWHERE, ANYWHERE],
        pltpu.VMEM((2 * rows, width // 2), data.dtype),
        IN_VMEM,
        [pltpu.SemaphoreType.DMA((2, BLOCKS))],
        0,
        rows * width * 4,
    )


def part_dots(start, groups, held, before, last):
    sizes = [g[0].shape[0] for g in groups]
    rows = sum(p.shape[1] for p in groups[0])
    block = groups[0][0].shape[2]
    both = held.shape[0]
    inner = both // 2
    parts = [p for g in groups for p in g]
    per = len(groups[0])
    height = rows // per
    spots = [(a, i) for a, size in enumerate(sizes) for i in range(size)]

    def kernel(*refs):
        pieces, (held_ref, *rest) = refs[: len(parts)], refs[len(parts) :]
        for p in range(per):
            here = pl.ds(p * height, height)
            total = None if before is None else rest[0][here]
            for t, (a, i) in enumerate(spots):
                part = lax.dot_general(
                    pieces[a * per + p][i],
                    held_ref[:, (start + t) * block : (start + t + 1) * block],
                    (((1,), (1,)), ((), ())),
                    preferred_element_type=jnp.float32,
                )
                total = part if total is None else total + part
            if last:
                rest[-2][here] = total[:, :inner]
                rest[-1][here] = total[:, inner:]
            else:
                rest[-1][here] = total

    ins = parts + [held] + ([] if before is None else [before])
    half = jax.ShapeDtypeStruct((rows, inner), jnp.float32)
    outs = [half, half] if last else [jax.ShapeDtypeStruct((rows, both), jnp.float32)]
    got = call(
        kernel,
        ins,
        [IN_VMEM] * len(ins),
        outs,
        [IN_VMEM] * len(outs),
        [],
        len(spots) * 2 * rows * both * block,
        len(spots) * block * 2 * (both + rows),
    )
    return got if len(got) > 1 else got[0]


def gathered_dots(noise, held, sq_data):
    half = noise.shape[0] // 2
    along = [hop(noise, -k, True) for k in OFFS] + [noise]
    top = jnp.stack([block[:half] for block in along])
    bottom = jnp.stack([block[half:] for block in along])
    top, bottom, sq_data = lax.optimization_barrier((top, bottom, sq_data))
    up_top, down_bottom = hop(top, -1, False), hop(bottom, 1, False)
    up_bottom, down_top = hop(bottom, -1, False), hop(top, 1, False)
    groups = [[block[None]] for block in along]
    dots = part_dots(0, groups, held, None, False)
    up_top, down_bottom, dots = lax.optimization_barrier((up_top, down_bottom, dots))
    far = [hop(up_top, -1, False), hop(down_bottom, 1, False)]
    groups = [[up_top, up_bottom], [down_top, down_bottom]]
    dots = part_dots(4, groups, held, dots, False)
    own, other = part_dots(12, [far], held, dots, True)
    return own + swap(other), sq_data


def part_sums(start, n, ins, ids, step=2):
    w_own, w_oth, data, data_other = ins
    rows, inner = w_own.shape
    dtype = data.dtype
    block = data.shape[1] // (2 * BLOCKS)
    half = rows // 2
    groups = len(start)

    def kernel(ids_ref, w_own_ref, w_oth_ref, data_ref, data_other_ref, *refs):
        outs, (weights, held, totals, in_sems, sems) = (
            refs[: 2 * groups],
            refs[2 * groups :],
        )
        into = []
        for a, first in enumerate(start):
            for i in range(n):
                into.append(
                    block_copies(
                        ids_ref,
                        first + i,
                        (data_ref, data_other_ref),
                        held,
                        a * n + i,
                        in_sems,
                    )
                )
                for copy in into[-1]:
                    copy.start()
        weights[:, :inner] = w_own_ref[...]
        weights[:, inner:] = w_oth_ref[...]
        out = []
        for a in range(groups):
            for i in range(0, n, step):
                spot = a * n + i
                for copies in into[spot : spot + step]:
                    for copy in copies:
                        copy.wait()
                total = jnp.dot(
                    weights[...],
                    held[:, spot * block : (spot + step) * block],
                    preferred_element_type=jnp.float32,
                ).astype(dtype)
                for j in range(step):
                    part = total[:, j * block : (j + 1) * block]
                    totals[2 * a, i + j] = part[:half]
                    totals[2 * a + 1, i + j] = part[half:]
            for p in range(2 * a, 2 * a + 2):
                out.append(pltpu.make_async_copy(totals.at[p], outs[p], sems.at[p]))
                out[-1].start()
        for copy in out:
            copy.wait()

    return call(
        kernel,
        [ids, w_own, w_oth] + in_hbm([data, data_other]),
        [IN_SMEM, IN_VMEM, IN_VMEM, ANYWHERE, ANYWHERE],
        [jax.ShapeDtypeStruct((n, half, block), dtype)] * (2 * groups),
        [ANYWHERE] * (2 * groups),
        [
            pltpu.VMEM((rows, 2 * inner), dtype),
            pltpu.VMEM((2 * inner, groups * n * block), dtype),
            pltpu.VMEM((2 * groups, n, half, block), dtype),
            pltpu.SemaphoreType.DMA((2, groups * n)),
            pltpu.SemaphoreType.DMA((2 * groups,)),
        ],
        groups * n * 4 * rows * inner * block,
        groups * n * 2 * block * (2 * inner + rows),
    )


def added(first, others):
    total = first.astype(jnp.float32)
    for other in others:
        total += other.astype(jnp.float32)
    return total


def scattered_sums(ins, ids, row_part):
    top, bottom = part_sums([12], 4, ins, ids)
    weights, top, bottom = lax.optimization_barrier((ins[0], top, bottom))
    ins = (weights,) + ins[1:]
    top, bottom = hop(top, 1, False), hop(bottom, -1, False)
    up_top, up_bottom, down_top, down_bottom = part_sums([4, 8], 4, ins, ids)
    weights, up_bottom, down_top = lax.optimization_barrier(
        (weights, up_bottom, down_top)
    )
    ins = (weights,) + ins[1:]
    tops, bottoms = [hop(down_top, -1, False)], [hop(up_bottom, 1, False)]
    near_top, near_bottom = part_sums([0], 4, ins, ids)
    tops.append(hop(added(up_top, [top]).astype(top.dtype), 1, False))
    bottoms.append(hop(added(down_bottom, [bottom]).astype(top.dtype), -1, False))
    totals = []
    for a in range(3):
        total = [
            added(near_top[a], [got[a] for got in tops]),
            added(near_bottom[a], [got[a] for got in bottoms]),
        ]
        totals.append(jnp.concatenate(total).astype(top.dtype))
    row_part, *totals = lax.optimization_barrier((row_part, *totals))
    sums = [hop(total, k, True) for total, k in zip(totals, OFFS)]
    row_sum = jnp.sum(to_all_dp(row_part), axis=0)
    row_sum, near_top = lax.optimization_barrier((row_sum, near_top))
    total = [
        added(near_top[3], [got[3] for got in tops]),
        added(near_bottom[3], [got[3] for got in bottoms]),
    ]
    return added(jnp.concatenate(total), sums), row_sum


def body(noise_latents, data_latents):
    width = data_latents.shape[1]
    place = lax.axis_index("dp")
    core = place % 2
    z = (place // 2) % SIDE
    y = place // (2 * SIDE)
    ids = block_ids(y, z, core)
    data_other = swap(data_latents)
    held = held_blocks(ids, data_latents, data_other)
    noise_f = noise_latents.astype(jnp.float32)
    sx_part = jnp.sum(noise_f * noise_f, axis=1)
    data_f = data_latents.astype(jnp.float32)
    sq_data = jnp.sum(data_f * data_f, axis=1)
    dots, sq_data = gathered_dots(noise_latents, held, sq_data)
    scale = 1.0 / (width * EPS)
    twice = dots * (2.0 * scale)
    sy = sq_data * scale
    sx = None
    g = jnp.zeros_like(sy)
    for step in range(ITERS):
        local = lse(twice + (g - sy)[None, :], 1)
        if sx is None:
            got = to_all_dp(jnp.stack([local, sx_part]))
            sx = jnp.sum(got[:, 1], axis=0) * scale
            got = got[:, 0]
        else:
            got = to_all_dp(local)
        f = sx - lse(got, 0)
        local = lse(twice + (f - sx)[:, None], 0)
        g = sy - lse(to_all_noise(local), 0)
    coupling = jnp.exp(twice + (f - sx)[:, None] + (g - sy)[None, :])
    weights = coupling.astype(jnp.bfloat16)
    total, row_sum = scattered_sums(
        (weights, swap(weights), data_latents, data_other),
        ids,
        jnp.sum(coupling, axis=1),
    )
    return (total / row_sum[:, None]).astype(jnp.bfloat16)


def solution(mesh):
    return jax.shard_map(
        body,
        mesh=mesh,
        in_specs=(P("noise", "dp"), P("dp", None)),
        out_specs=P("noise", "dp"),
        check_vma=False,
    )
```

```python
import jax
import jax.numpy as jnp
from jax import lax
from jax.experimental import pallas as pl
from jax.experimental.pallas import tpu as pltpu
from jax.sharding import PartitionSpec as P

ITERS = 3
EPS = 0.004
SIDE = 4
OFFS = (2, 1, 3)
BLOCKS = SIDE * SIDE
EXTRA = 16
VMEM_LIMIT = 24 * 1024 * 1024

SPOTS = [(k, m) for k in (0, 1, 3, 2) for m in OFFS + (0,)]


def swap(values):
    n = lax.axis_size("dp")
    return lax.ppermute(values, "dp", [(i, i ^ 1) for i in range(n)])


def hop(values, k, first):
    pairs = []
    for y in range(SIDE):
        for z in range(SIDE):
            for c in range(2):
                along_z = (c == 0) == first
                to_y, to_z = (y, (z + k) % SIDE) if along_z else ((y + k) % SIDE, z)
                pairs.append(((y * SIDE + z) * 2 + c, (to_y * SIDE + to_z) * 2 + c))
    return lax.ppermute(values, "dp", pairs)


def block_ids(y, z, core):
    ids = []
    for k, m in SPOTS:
        dy = jnp.where(core == 0, k, m)
        dz = jnp.where(core == 0, m, k)
        ids.append((((y + dy) % SIDE) * SIDE + (z + dz) % SIDE) * 2 + core)
    return jnp.stack(ids).astype(jnp.int32)


def lse(values, axis):
    peak = jnp.max(values, axis=axis, keepdims=True)
    total = jnp.sum(jnp.exp(values - peak), axis=axis)
    return jnp.squeeze(peak, axis) + jnp.log(total)


def to_all_dp(values):
    n = lax.axis_size("dp")
    return lax.all_to_all(
        jnp.broadcast_to(values[None], (n,) + values.shape), "dp", 0, 0
    )


def to_all_noise(values):
    n = lax.axis_size("noise")
    parts = [values]
    for k in range(1, n):
        parts.append(
            lax.ppermute(values, "noise", [(i, (i + k) % n) for i in range(n)])
        )
    return jnp.stack(parts)


def call(kernel, ins, in_specs, out_shape, out_specs, scratch, flops, moved):
    return pl.pallas_call(
        kernel,
        in_specs=in_specs,
        out_specs=out_specs,
        out_shape=out_shape,
        scratch_shapes=scratch,
        compiler_params=pltpu.CompilerParams(vmem_limit_bytes=VMEM_LIMIT),
        cost_estimate=pl.CostEstimate(
            flops=flops, bytes_accessed=moved, transcendentals=0
        ),
    )(*ins)


IN_SMEM = pl.BlockSpec(memory_space=pltpu.SMEM)
IN_VMEM = pl.BlockSpec(memory_space=pltpu.VMEM)
ANYWHERE = pl.BlockSpec(memory_space=pl.ANY)


def in_hbm(arrays):
    return [pltpu.with_memory_space_constraint(a, pltpu.HBM) for a in arrays]


def block_copies(ids_ref, t, refs, to, spot, sems):
    rows, width = refs[0].shape
    block = width // (2 * BLOCKS)
    place = pl.multiple_of(ids_ref[t] * block, block)
    return [
        pltpu.make_async_copy(
            ref.at[:, pl.ds(place, block)],
            to.at[pl.ds(b * rows, rows), pl.ds(spot * block, block)],
            sems.at[b, spot],
        )
        for b, ref in enumerate(refs)
    ]


def held_blocks(ids, data, data_other):
    rows, width = data.shape

    def kernel(ids_ref, data_ref, data_other_ref, held, sems):
        copies = []
        for t in range(BLOCKS):
            copies += block_copies(
                ids_ref, t, (data_ref, data_other_ref), held, t, sems
            )
        for copy in copies:
            copy.start()
        for copy in copies:
            copy.wait()

    return call(
        kernel,
        [ids] + in_hbm([data, data_other]),
        [IN_SMEM, ANYWHERE, ANYWHERE],
        pltpu.VMEM((2 * rows, width // 2), data.dtype),
        IN_VMEM,
        [pltpu.SemaphoreType.DMA((2, BLOCKS))],
        0,
        rows * width * 4,
    )


def part_dots(start, groups, held, before, last):
    sizes = [g[0].shape[0] for g in groups]
    rows = sum(p.shape[1] for p in groups[0])
    block = groups[0][0].shape[2]
    both = held.shape[0]
    inner = both // 2
    parts = [p for g in groups for p in g]
    per = len(groups[0])
    height = rows // per
    spots = [(a, i) for a, size in enumerate(sizes) for i in range(size)]

    def kernel(*refs):
        pieces, (held_ref, *rest) = refs[: len(parts)], refs[len(parts) :]
        for p in range(per):
            here = pl.ds(p * height, height)
            total = None if before is None else rest[0][here]
            for t, (a, i) in enumerate(spots):
                part = lax.dot_general(
                    pieces[a * per + p][i],
                    held_ref[:, (start + t) * block : (start + t + 1) * block],
                    (((1,), (1,)), ((), ())),
                    preferred_element_type=jnp.float32,
                )
                total = part if total is None else total + part
            if last:
                rest[-2][here] = total[:, :inner]
                rest[-1][here] = total[:, inner:]
            else:
                rest[-1][here] = total

    ins = parts + [held] + ([] if before is None else [before])
    half = jax.ShapeDtypeStruct((rows, inner), jnp.float32)
    outs = [half, half] if last else [jax.ShapeDtypeStruct((rows, both), jnp.float32)]
    got = call(
        kernel,
        ins,
        [IN_VMEM] * len(ins),
        outs,
        [IN_VMEM] * len(outs),
        [],
        len(spots) * 2 * rows * both * block,
        len(spots) * block * 2 * (both + rows),
    )
    return got if len(got) > 1 else got[0]


def gathered_dots(noise, held, sq_data):
    half = noise.shape[0] // 2
    along = [hop(noise, -k, True) for k in OFFS] + [noise]
    top = jnp.stack([block[:half] for block in along])
    bottom = jnp.stack([block[half:] for block in along])
    top, bottom, sq_data = lax.optimization_barrier((top, bottom, sq_data))
    up_top, down_bottom = hop(top, -1, False), hop(bottom, 1, False)
    up_bottom, down_top = hop(bottom, -1, False), hop(top, 1, False)
    groups = [[block[None]] for block in along]
    dots = part_dots(0, groups, held, None, False)
    up_top, down_bottom, dots = lax.optimization_barrier((up_top, down_bottom, dots))
    far = [hop(up_top, -1, False), hop(down_bottom, 1, False)]
    groups = [[up_top, up_bottom], [down_top, down_bottom]]
    dots = part_dots(4, groups, held, dots, False)
    own, other = part_dots(12, [far], held, dots, True)
    return own + swap(other), sq_data


def part_sums(start, n, ins, ids, step=2):
    w_own, w_oth, data, data_other = ins
    rows, inner = w_own.shape
    dtype = data.dtype
    block = data.shape[1] // (2 * BLOCKS)
    half = rows // 2
    groups = len(start)

    def kernel(ids_ref, w_own_ref, w_oth_ref, data_ref, data_other_ref, *refs):
        outs, (weights, held, tops, bottoms, in_sems, sems) = (
            refs[: 2 * groups],
            refs[2 * groups :],
        )
        into = []
        for a, first in enumerate(start):
            for i in range(n):
                into.append(
                    block_copies(
                        ids_ref,
                        first + i,
                        (data_ref, data_other_ref),
                        held,
                        a * n + i,
                        in_sems,
                    )
                )
                for copy in into[-1]:
                    copy.start()
        weights[:, :inner] = w_own_ref[...]
        weights[:, inner:] = w_oth_ref[...]
        ones = jnp.ones((EXTRA, 2 * inner), dtype)
        row_sums = lax.dot_general(
            ones,
            weights[...],
            (((1,), (1,)), ((), ())),
            preferred_element_type=jnp.float32,
        ).astype(dtype)
        out = []
        for a in range(groups):
            for i in range(n):
                tops[a, i, half:, :rows] = row_sums
                tops[a, i, half:, rows:] = jnp.zeros((EXTRA, block - rows), dtype)
            for i in range(0, n, step):
                spot = a * n + i
                for copies in into[spot : spot + step]:
                    for copy in copies:
                        copy.wait()
                total = jnp.dot(
                    weights[...],
                    held[:, spot * block : (spot + step) * block],
                    preferred_element_type=jnp.float32,
                ).astype(dtype)
                for j in range(step):
                    part = total[:, j * block : (j + 1) * block]
                    tops[a, i + j, :half] = part[:half]
                    bottoms[a, i + j] = part[half:]
            for p, held_part in enumerate((tops, bottoms)):
                to = 2 * a + p
                out.append(
                    pltpu.make_async_copy(held_part.at[a], outs[to], sems.at[to])
                )
                out[-1].start()
        for copy in out:
            copy.wait()

    return call(
        kernel,
        [ids, w_own, w_oth] + in_hbm([data, data_other]),
        [IN_SMEM, IN_VMEM, IN_VMEM, ANYWHERE, ANYWHERE],
        [
            jax.ShapeDtypeStruct((n, half + EXTRA, block), dtype),
            jax.ShapeDtypeStruct((n, half, block), dtype),
        ]
        * groups,
        [ANYWHERE] * (2 * groups),
        [
            pltpu.VMEM((rows, 2 * inner), dtype),
            pltpu.VMEM((2 * inner, groups * n * block), dtype),
            pltpu.VMEM((groups, n, half + EXTRA, block), dtype),
            pltpu.VMEM((groups, n, half, block), dtype),
            pltpu.SemaphoreType.DMA((2, groups * n)),
            pltpu.SemaphoreType.DMA((2 * groups,)),
        ],
        groups * n * 4 * rows * inner * block,
        groups * n * 2 * block * (2 * inner + rows),
    )


def added(first, others):
    total = first.astype(jnp.float32)
    for other in others:
        total += other.astype(jnp.float32)
    return total


def scattered_sums(ins, ids):
    top, bottom = part_sums([12], 4, ins, ids)
    weights, top, bottom = lax.optimization_barrier((ins[0], top, bottom))
    ins = (weights,) + ins[1:]
    top, bottom = hop(top, 1, False), hop(bottom, -1, False)
    up_top, up_bottom, down_top, down_bottom = part_sums([4, 8], 4, ins, ids)
    weights, up_bottom, down_top = lax.optimization_barrier(
        (weights, up_bottom, down_top)
    )
    ins = (weights,) + ins[1:]
    tops, bottoms = [hop(down_top, -1, False)], [hop(up_bottom, 1, False)]
    near_top, near_bottom = part_sums([0], 4, ins, ids)
    tops.append(hop(added(up_top, [top]).astype(top.dtype), 1, False))
    bottoms.append(hop(added(down_bottom, [bottom]).astype(top.dtype), -1, False))
    totals = []
    for a in range(3):
        total = [
            added(near_top[a], [got[a] for got in tops]),
            added(near_bottom[a], [got[a] for got in bottoms]),
        ]
        totals.append(jnp.concatenate(total).astype(top.dtype))
    last = [hop(total, k, True) for total, k in zip(totals, OFFS)]
    total = [
        added(near_top[3], [got[3] for got in tops]),
        added(near_bottom[3], [got[3] for got in bottoms]),
    ]
    total = added(jnp.concatenate(total), last)
    rows = total.shape[0] - EXTRA
    half = rows // 2
    row_sums = total[half, :rows]
    means = jnp.concatenate([total[:half], total[half + EXTRA :]])
    return means / row_sums[:, None]


def body(noise_latents, data_latents):
    width = data_latents.shape[1]
    place = lax.axis_index("dp")
    core = place % 2
    z = (place // 2) % SIDE
    y = place // (2 * SIDE)
    ids = block_ids(y, z, core)
    data_other = swap(data_latents)
    held = held_blocks(ids, data_latents, data_other)
    noise_f = noise_latents.astype(jnp.float32)
    sx_part = jnp.sum(noise_f * noise_f, axis=1)
    data_f = data_latents.astype(jnp.float32)
    sq_data = jnp.sum(data_f * data_f, axis=1)
    dots, sq_data = gathered_dots(noise_latents, held, sq_data)
    scale = 1.0 / (width * EPS)
    twice = dots * (2.0 * scale)
    sy = sq_data * scale
    sx = None
    g = jnp.zeros_like(sy)
    for step in range(ITERS):
        local = lse(twice + (g - sy)[None, :], 1)
        if sx is None:
            got = to_all_dp(jnp.stack([local, sx_part]))
            sx = jnp.sum(got[:, 1], axis=0) * scale
            got = got[:, 0]
        else:
            got = to_all_dp(local)
        f = sx - lse(got, 0)
        local = lse(twice + (f - sx)[:, None], 0)
        g = sy - lse(to_all_noise(local), 0)
    coupling = jnp.exp(twice + (f - sx)[:, None] + (g - sy)[None, :])
    weights = coupling.astype(jnp.bfloat16)
    means = scattered_sums(
        (weights, swap(weights), data_latents, data_other), ids
    )
    return means.astype(jnp.bfloat16)


def solution(mesh):
    return jax.shard_map(
        body,
        mesh=mesh,
        in_specs=(P("noise", "dp"), P("dp", None)),
        out_specs=P("noise", "dp"),
        check_vma=False,
    )
```

```python
import jax
import jax.numpy as jnp
from jax import lax
from jax.experimental import pallas as pl
from jax.experimental.pallas import tpu as pltpu
from jax.sharding import PartitionSpec as P

ITERS = 3
EPS = 0.004
SIDE = 4
OFFS = (2, 1, 3)
BLOCKS = SIDE * SIDE
EXTRA = 16
VMEM_LIMIT = 24 * 1024 * 1024

SPOTS = [(k, m) for k in (0, 1, 3, 2) for m in OFFS + (0,)]


def swap(values):
    n = lax.axis_size("dp")
    return lax.ppermute(values, "dp", [(i, i ^ 1) for i in range(n)])


def hop(values, k, first):
    pairs = []
    for y in range(SIDE):
        for z in range(SIDE):
            for c in range(2):
                along_z = (c == 0) == first
                to_y, to_z = (y, (z + k) % SIDE) if along_z else ((y + k) % SIDE, z)
                pairs.append(((y * SIDE + z) * 2 + c, (to_y * SIDE + to_z) * 2 + c))
    return lax.ppermute(values, "dp", pairs)


def block_ids(y, z, core):
    ids = []
    for k, m in SPOTS:
        dy = jnp.where(core == 0, k, m)
        dz = jnp.where(core == 0, m, k)
        ids.append((((y + dy) % SIDE) * SIDE + (z + dz) % SIDE) * 2 + core)
    return jnp.stack(ids).astype(jnp.int32)


def lse(values, axis):
    peak = jnp.max(values, axis=axis, keepdims=True)
    total = jnp.sum(jnp.exp(values - peak), axis=axis)
    return jnp.squeeze(peak, axis) + jnp.log(total)


def to_all_dp(values):
    n = lax.axis_size("dp")
    return lax.all_to_all(
        jnp.broadcast_to(values[None], (n,) + values.shape), "dp", 0, 0
    )


def to_all_noise(values):
    n = lax.axis_size("noise")
    parts = [values]
    for k in sorted(range(1, n), key=lambda k: -min(k, n - k)):
        parts.append(
            lax.ppermute(values, "noise", [(i, (i + k) % n) for i in range(n)])
        )
    return jnp.stack(parts)


def call(kernel, ins, in_specs, out_shape, out_specs, scratch, flops, moved):
    return pl.pallas_call(
        kernel,
        in_specs=in_specs,
        out_specs=out_specs,
        out_shape=out_shape,
        scratch_shapes=scratch,
        compiler_params=pltpu.CompilerParams(vmem_limit_bytes=VMEM_LIMIT),
        cost_estimate=pl.CostEstimate(
            flops=flops, bytes_accessed=moved, transcendentals=0
        ),
    )(*ins)


IN_SMEM = pl.BlockSpec(memory_space=pltpu.SMEM)
IN_VMEM = pl.BlockSpec(memory_space=pltpu.VMEM)
ANYWHERE = pl.BlockSpec(memory_space=pl.ANY)


def in_hbm(arrays):
    return [pltpu.with_memory_space_constraint(a, pltpu.HBM) for a in arrays]


def block_copies(ids_ref, t, refs, to, spot, sems):
    rows, width = refs[0].shape
    block = width // (2 * BLOCKS)
    place = pl.multiple_of(ids_ref[t] * block, block)
    return [
        pltpu.make_async_copy(
            ref.at[:, pl.ds(place, block)],
            to.at[pl.ds(b * rows, rows), pl.ds(spot * block, block)],
            sems.at[b, spot],
        )
        for b, ref in enumerate(refs)
    ]


def held_blocks(ids, start, n, data, data_other):
    rows, width = data.shape
    block = width // (2 * BLOCKS)

    def kernel(ids_ref, data_ref, data_other_ref, held, sems):
        copies = []
        for t in range(n):
            copies += block_copies(
                ids_ref, start + t, (data_ref, data_other_ref), held, t, sems
            )
        for copy in copies:
            copy.start()
        for copy in copies:
            copy.wait()

    return call(
        kernel,
        [ids] + in_hbm([data, data_other]),
        [IN_SMEM, ANYWHERE, ANYWHERE],
        pltpu.VMEM((2 * rows, n * block), data.dtype),
        IN_VMEM,
        [pltpu.SemaphoreType.DMA((2, n))],
        0,
        n * rows * block * 8,
    )


def part_dots(start, groups, held, before, last):
    sizes = [g[0].shape[0] for g in groups]
    rows = sum(p.shape[1] for p in groups[0])
    block = groups[0][0].shape[2]
    both = held.shape[0]
    inner = both // 2
    parts = [p for g in groups for p in g]
    per = len(groups[0])
    height = rows // per
    spots = [(a, i) for a, size in enumerate(sizes) for i in range(size)]

    def kernel(*refs):
        pieces, (held_ref, *rest) = refs[: len(parts)], refs[len(parts) :]
        for p in range(per):
            here = pl.ds(p * height, height)
            total = None if before is None else rest[0][here]
            for t, (a, i) in enumerate(spots):
                part = lax.dot_general(
                    pieces[a * per + p][i],
                    held_ref[:, (start + t) * block : (start + t + 1) * block],
                    (((1,), (1,)), ((), ())),
                    preferred_element_type=jnp.float32,
                )
                total = part if total is None else total + part
            if last:
                rest[-2][here] = total[:, :inner]
                rest[-1][here] = total[:, inner:]
            else:
                rest[-1][here] = total

    ins = parts + [held] + ([] if before is None else [before])
    half = jax.ShapeDtypeStruct((rows, inner), jnp.float32)
    outs = [half, half] if last else [jax.ShapeDtypeStruct((rows, both), jnp.float32)]
    got = call(
        kernel,
        ins,
        [IN_VMEM] * len(ins),
        outs,
        [IN_VMEM] * len(outs),
        [],
        len(spots) * 2 * rows * both * block,
        len(spots) * block * 2 * (both + rows),
    )
    return got if len(got) > 1 else got[0]


def gathered_dots(noise, held, sq_data):
    half = noise.shape[0] // 2
    along = [hop(noise, -k, True) for k in OFFS] + [noise]
    top = jnp.stack([block[:half] for block in along])
    bottom = jnp.stack([block[half:] for block in along])
    top, bottom, sq_data = lax.optimization_barrier((top, bottom, sq_data))
    up_top, down_bottom = hop(top, -1, False), hop(bottom, 1, False)
    up_bottom, down_top = hop(bottom, -1, False), hop(top, 1, False)
    groups = [[block[None]] for block in along]
    dots = part_dots(0, groups, held, None, False)
    up_top, down_bottom, dots = lax.optimization_barrier((up_top, down_bottom, dots))
    far = [hop(up_top, -1, False), hop(down_bottom, 1, False)]
    groups = [[up_top, up_bottom], [down_top, down_bottom]]
    dots = part_dots(4, groups, held, dots, False)
    own, other = part_dots(12, [far], held, dots, True)
    return own + swap(other), sq_data


def part_sums(start, groups, ins, ids, ready=None, step=2):
    w_own, w_oth, data, data_other = ins
    rows, inner = w_own.shape
    dtype = data.dtype
    block = data.shape[1] // (2 * BLOCKS)
    half = rows // 2
    ends = [sum(groups[: a + 1]) for a in range(len(groups))]
    count = ends[-1]
    sources = [data, data_other] if ready is None else [ready]

    def kernel(ids_ref, w_own_ref, w_oth_ref, *refs):
        refs, outs, scratch = (
            refs[: len(sources)],
            refs[len(sources) : len(sources) + 2 * len(groups)],
            refs[len(sources) + 2 * len(groups) :],
        )
        weights, tops, bottoms, sems, *scratch = scratch
        into = [[]] * count
        if ready is None:
            held, in_sems = scratch
            into = [
                block_copies(ids_ref, start + spot, refs, held, spot, in_sems)
                for spot in range(count)
            ]
            for copies in into:
                for copy in copies:
                    copy.start()
        else:
            (held,) = refs
        weights[:, :inner] = w_own_ref[...]
        weights[:, inner:] = w_oth_ref[...]
        ones = jnp.ones((EXTRA, 2 * inner), dtype)
        row_sums = lax.dot_general(
            ones,
            weights[...],
            (((1,), (1,)), ((), ())),
            preferred_element_type=jnp.float32,
        ).astype(dtype)
        for spot in range(count):
            tops[spot, half:, :rows] = row_sums
            tops[spot, half:, rows:] = jnp.zeros((EXTRA, block - rows), dtype)
        out = []
        for spot in range(0, count, step):
            stop = spot + step
            for copies in into[spot:stop]:
                for copy in copies:
                    copy.wait()
            total = jnp.dot(
                weights[...],
                held[:, spot * block : stop * block],
                preferred_element_type=jnp.float32,
            ).astype(dtype)
            for j in range(step):
                part = total[:, j * block : (j + 1) * block]
                tops[spot + j, :half] = part[:half]
                bottoms[spot + j] = part[half:]
            for a, n in enumerate(groups):
                if not spot < ends[a] <= stop:
                    continue
                for p, source in enumerate((tops, bottoms)):
                    to = 2 * a + p
                    out.append(
                        pltpu.make_async_copy(
                            source.at[pl.ds(ends[a] - n, n)], outs[to], sems.at[to]
                        )
                    )
                    out[-1].start()
        for copy in out:
            copy.wait()

    shapes = []
    for n in groups:
        shapes.append(jax.ShapeDtypeStruct((n, half + EXTRA, block), dtype))
        shapes.append(jax.ShapeDtypeStruct((n, half, block), dtype))
    scratch = [
        pltpu.VMEM((rows, 2 * inner), dtype),
        pltpu.VMEM((count, half + EXTRA, block), dtype),
        pltpu.VMEM((count, half, block), dtype),
        pltpu.SemaphoreType.DMA((2 * len(groups),)),
    ]
    if ready is None:
        scratch.append(pltpu.VMEM((2 * inner, count * block), dtype))
        scratch.append(pltpu.SemaphoreType.DMA((2, count)))
        sources = in_hbm(sources)
    return call(
        kernel,
        [ids, w_own, w_oth] + sources,
        [IN_SMEM, IN_VMEM, IN_VMEM]
        + ([ANYWHERE] * 2 if ready is None else [IN_VMEM]),
        shapes,
        [ANYWHERE] * len(shapes),
        scratch,
        count * 4 * rows * inner * block,
        count * 2 * block * (2 * inner + rows),
    )


def added(first, others):
    total = first.astype(jnp.float32)
    for other in others:
        total += other.astype(jnp.float32)
    return total


def scattered_sums(ins, ids, ready):
    top, bottom = part_sums(12, [4], ins, ids, ready)
    weights, top, bottom = lax.optimization_barrier((ins[0], top, bottom))
    ins = (weights,) + ins[1:]
    top, bottom = hop(top, 1, False), hop(bottom, -1, False)
    parts = part_sums(4, [3, 1, 3, 1], ins, ids)
    up_top, up_bottom, up_own_top, up_own_bottom, *parts = parts
    down_top, down_bottom, down_own_top, down_own_bottom = parts
    tops, bottoms = [hop(down_top, -1, False)], [hop(up_bottom, 1, False)]
    dtype = top.dtype
    up_top = added(up_top, [top[:3]]).astype(dtype)
    down_bottom = added(down_bottom, [bottom[:3]]).astype(dtype)
    weights, up_top, down_bottom = lax.optimization_barrier(
        (weights, up_top, down_bottom)
    )
    tops.append(hop(up_top, 1, False))
    bottoms.append(hop(down_bottom, -1, False))
    ins = (weights,) + ins[1:]
    near_top, near_bottom = part_sums(0, [4], ins, ids)
    up_own_top = added(up_own_top[0], [top[3]]).astype(dtype)
    down_own_bottom = added(down_own_bottom[0], [bottom[3]]).astype(dtype)
    last = [
        hop(jnp.concatenate([up_own_top, up_own_bottom[0]]), 1, False),
        hop(jnp.concatenate([down_own_top[0], down_own_bottom]), -1, False),
    ]
    for a, k in enumerate(OFFS):
        total = [
            added(near_top[a], [got[a] for got in tops]),
            added(near_bottom[a], [got[a] for got in bottoms]),
        ]
        last.append(hop(jnp.concatenate(total).astype(dtype), k, True))
    total = added(jnp.concatenate([near_top[3], near_bottom[3]]), last)
    rows = total.shape[0] - EXTRA
    half = rows // 2
    row_sums = total[half, :rows]
    means = jnp.concatenate([total[:half], total[half + EXTRA :]])
    return means / row_sums[:, None]


def body(noise_latents, data_latents):
    width = data_latents.shape[1]
    place = lax.axis_index("dp")
    core = place % 2
    z = (place // 2) % SIDE
    y = place // (2 * SIDE)
    ids = block_ids(y, z, core)
    data_other = swap(data_latents)
    held = held_blocks(ids, 0, BLOCKS, data_latents, data_other)
    noise_f = noise_latents.astype(jnp.float32)
    sx_part = jnp.sum(noise_f * noise_f, axis=1)
    data_f = data_latents.astype(jnp.float32)
    sq_data = jnp.sum(data_f * data_f, axis=1)
    dots, sq_data = gathered_dots(noise_latents, held, sq_data)
    scale = 1.0 / (width * EPS)
    twice = dots * (2.0 * scale)
    sy = sq_data * scale
    sx = None
    g = jnp.zeros_like(sy)
    for step in range(ITERS):
        local = lse(twice + (g - sy)[None, :], 1)
        if sx is None:
            got = to_all_dp(jnp.stack([local, sx_part]))
            sx = jnp.sum(got[:, 1], axis=0) * scale
            got = got[:, 0]
        else:
            got = to_all_dp(local)
        f = sx - lse(got, 0)
        local = lse(twice + (f - sx)[:, None], 0)
        if step == ITERS - 1:
            local, ids = lax.optimization_barrier((local, ids))
        g = sy - lse(to_all_noise(local), 0)
    coupling = jnp.exp(twice + (f - sx)[:, None] + (g - sy)[None, :])
    weights = coupling.astype(jnp.bfloat16)
    ready = held_blocks(ids, 12, 4, data_latents, data_other)
    means = scattered_sums(
        (weights, swap(weights), data_latents, data_other), ids, ready
    )
    return means.astype(jnp.bfloat16)


def solution(mesh):
    return jax.shard_map(
        body,
        mesh=mesh,
        in_specs=(P("noise", "dp"), P("dp", None)),
        out_specs=P("noise", "dp"),
        check_vma=False,
    )
```

```python
import jax
import jax.numpy as jnp
from jax import lax
from jax.experimental import pallas as pl
from jax.experimental.pallas import tpu as pltpu
from jax.sharding import PartitionSpec as P

ITERS = 3
EPS = 0.004
SIDE = 4
OFFS = (2, 1, 3)
BLOCKS = SIDE * SIDE
EXTRA = 16
VMEM_LIMIT = 14 * 1024 * 1024

SPOTS = [(k, m) for k in (0, 1, 3, 2) for m in OFFS + (0,)]


def swap(values):
    n = lax.axis_size("dp")
    return lax.ppermute(values, "dp", [(i, i ^ 1) for i in range(n)])


def hop(values, k, first):
    pairs = []
    for y in range(SIDE):
        for z in range(SIDE):
            for c in range(2):
                along_z = (c == 0) == first
                to_y, to_z = (y, (z + k) % SIDE) if along_z else ((y + k) % SIDE, z)
                pairs.append(((y * SIDE + z) * 2 + c, (to_y * SIDE + to_z) * 2 + c))
    return lax.ppermute(values, "dp", pairs)


def block_ids(y, z, core):
    ids = []
    for k, m in SPOTS:
        dy = jnp.where(core == 0, k, m)
        dz = jnp.where(core == 0, m, k)
        ids.append((((y + dy) % SIDE) * SIDE + (z + dz) % SIDE) * 2 + core)
    return jnp.stack(ids).astype(jnp.int32)


def lse(values, axis):
    peak = jnp.max(values, axis=axis, keepdims=True)
    total = jnp.sum(jnp.exp(values - peak), axis=axis)
    return jnp.squeeze(peak, axis) + jnp.log(total)


def to_all_dp(values):
    n = lax.axis_size("dp")
    return lax.all_to_all(
        jnp.broadcast_to(values[None], (n,) + values.shape), "dp", 0, 0
    )


def to_all_noise(values):
    n = lax.axis_size("noise")
    parts = [values]
    for k in sorted(range(1, n), key=lambda k: -min(k, n - k)):
        parts.append(
            lax.ppermute(values, "noise", [(i, (i + k) % n) for i in range(n)])
        )
    return jnp.stack(parts)


def call(kernel, ins, in_specs, out_shape, out_specs, scratch, flops, moved):
    return pl.pallas_call(
        kernel,
        in_specs=in_specs,
        out_specs=out_specs,
        out_shape=out_shape,
        scratch_shapes=scratch,
        compiler_params=pltpu.CompilerParams(vmem_limit_bytes=VMEM_LIMIT),
        cost_estimate=pl.CostEstimate(
            flops=flops, bytes_accessed=moved, transcendentals=0
        ),
    )(*ins)


IN_SMEM = pl.BlockSpec(memory_space=pltpu.SMEM)
IN_VMEM = pl.BlockSpec(memory_space=pltpu.VMEM)
ANYWHERE = pl.BlockSpec(memory_space=pl.ANY)


def in_hbm(arrays):
    return [pltpu.with_memory_space_constraint(a, pltpu.HBM) for a in arrays]


def block_copies(ids_ref, t, refs, to, spot, sems):
    rows, width = refs[0].shape
    block = width // (2 * BLOCKS)
    place = pl.multiple_of(ids_ref[t] * block, block)
    return [
        pltpu.make_async_copy(
            ref.at[:, pl.ds(place, block)],
            to.at[pl.ds(b * rows, rows), pl.ds(spot * block, block)],
            sems.at[b, spot],
        )
        for b, ref in enumerate(refs)
    ]


def held_blocks(ids, start, n, data, data_other):
    rows, width = data.shape
    block = width // (2 * BLOCKS)

    def kernel(ids_ref, data_ref, data_other_ref, held, mark, sems):
        copies = []
        for t in range(n):
            copies += block_copies(
                ids_ref, start + t, (data_ref, data_other_ref), held, t, sems
            )
        for copy in copies:
            copy.start()
        mark[...] = jnp.zeros_like(mark)
        for copy in copies:
            copy.wait()

    return call(
        kernel,
        [ids] + in_hbm([data, data_other]),
        [IN_SMEM, ANYWHERE, ANYWHERE],
        [
            pltpu.VMEM((2 * rows, n * block), data.dtype),
            jax.ShapeDtypeStruct((8, 128), jnp.float32),
        ],
        [IN_VMEM, IN_VMEM],
        [pltpu.SemaphoreType.DMA((2, n))],
        0,
        n * rows * block * 8,
    )


def part_dots(start, groups, held, before, side=None):
    rows, block = groups[0].shape[1:]
    both = held.shape[0]
    mine = slice(0, both)
    if side is not None:
        mine = slice(side * both // 2, (side + 1) * both // 2)
    width = mine.stop - mine.start
    spots = [(a, i) for a, g in enumerate(groups) for i in range(g.shape[0])]

    def kernel(*refs):
        pieces, (held_ref, *rest) = refs[: len(groups)], refs[len(groups) :]
        total = None if before is None else rest[0][:, mine]
        for t, (a, i) in enumerate(spots):
            part = lax.dot_general(
                pieces[a][i],
                held_ref[mine, (start + t) * block : (start + t + 1) * block],
                (((1,), (1,)), ((), ())),
                preferred_element_type=jnp.float32,
            )
            total = part if total is None else total + part
        rest[-1][...] = total

    ins = groups + [held] + ([] if before is None else [before])
    return call(
        kernel,
        ins,
        [IN_VMEM] * len(ins),
        jax.ShapeDtypeStruct((rows, width), jnp.float32),
        IN_VMEM,
        [],
        len(spots) * 2 * rows * width * block,
        len(spots) * block * 2 * (width + rows),
    )


def gathered_dots(noise, held, sq_data):
    along = [hop(noise, -k, True) for k in OFFS] + [noise]
    one, two = jnp.stack(along[:2]), jnp.stack(along[2:])
    one, two, sq_data = lax.optimization_barrier((one, two, sq_data))
    up_one, down_two = hop(one, -1, False), hop(two, 1, False)
    up_two, down_one = hop(two, -1, False), hop(one, 1, False)
    dots = part_dots(0, [one, two], held, None)
    up_one, down_two, dots = lax.optimization_barrier((up_one, down_two, dots))
    far = [hop(up_one, -1, False), hop(down_two, 1, False)]
    dots = part_dots(4, [up_one, up_two, down_one, down_two], held, dots)
    other = swap(part_dots(12, far, held, dots, 1))
    return part_dots(12, far, held, dots, 0) + other, sq_data


def part_sums(start, groups, ins, ids, ready=None, step=2):
    w_own, w_oth, data, data_other = ins
    rows, inner = w_own.shape
    dtype = data.dtype
    block = data.shape[1] // (2 * BLOCKS)
    half = rows // 2
    ends = [sum(groups[: a + 1]) for a in range(len(groups))]
    count = ends[-1]
    sources = [data, data_other] if ready is None else ready

    def kernel(ids_ref, w_own_ref, w_oth_ref, *refs):
        refs, outs, scratch = (
            refs[: len(sources)],
            refs[len(sources) : len(sources) + 2 * len(groups)],
            refs[len(sources) + 2 * len(groups) :],
        )
        weights, tops, bottoms, sems, *scratch = scratch
        into = [[]] * count
        if ready is None:
            held, in_sems = scratch
            into = [
                block_copies(ids_ref, start + spot, refs, held, spot, in_sems)
                for spot in range(count)
            ]
            for copies in into:
                for copy in copies:
                    copy.start()
        else:
            held, _ = refs
        weights[:, :inner] = w_own_ref[...]
        weights[:, inner:] = w_oth_ref[...]
        ones = jnp.ones((EXTRA, 2 * inner), dtype)
        row_sums = lax.dot_general(
            ones,
            weights[...],
            (((1,), (1,)), ((), ())),
            preferred_element_type=jnp.float32,
        ).astype(dtype)
        for spot in range(count):
            tops[spot, half:, :rows] = row_sums
            tops[spot, half:, rows:] = jnp.zeros((EXTRA, block - rows), dtype)
        out = []
        for spot in range(0, count, step):
            stop = spot + step
            for copies in into[spot:stop]:
                for copy in copies:
                    copy.wait()
            total = jnp.dot(
                weights[...],
                held[:, spot * block : stop * block],
                preferred_element_type=jnp.float32,
            ).astype(dtype)
            for j in range(step):
                part = total[:, j * block : (j + 1) * block]
                tops[spot + j, :half] = part[:half]
                bottoms[spot + j] = part[half:]
            for a, n in enumerate(groups):
                if not spot < ends[a] <= stop:
                    continue
                for p, source in enumerate((tops, bottoms)):
                    to = 2 * a + p
                    out.append(
                        pltpu.make_async_copy(
                            source.at[pl.ds(ends[a] - n, n)], outs[to], sems.at[to]
                        )
                    )
                    out[-1].start()
        for copy in out:
            copy.wait()

    shapes = []
    for n in groups:
        shapes.append(jax.ShapeDtypeStruct((n, half + EXTRA, block), dtype))
        shapes.append(jax.ShapeDtypeStruct((n, half, block), dtype))
    scratch = [
        pltpu.VMEM((rows, 2 * inner), dtype),
        pltpu.VMEM((count, half + EXTRA, block), dtype),
        pltpu.VMEM((count, half, block), dtype),
        pltpu.SemaphoreType.DMA((2 * len(groups),)),
    ]
    if ready is None:
        scratch.append(pltpu.VMEM((2 * inner, count * block), dtype))
        scratch.append(pltpu.SemaphoreType.DMA((2, count)))
        sources = in_hbm(sources)
    return call(
        kernel,
        [ids, w_own, w_oth] + sources,
        [IN_SMEM, IN_VMEM, IN_VMEM]
        + [ANYWHERE if ready is None else IN_VMEM] * 2,
        shapes,
        [ANYWHERE] * len(shapes),
        scratch,
        count * 4 * rows * inner * block,
        count * 2 * block * (2 * inner + rows),
    )


def added(first, others):
    total = first.astype(jnp.float32)
    for other in others:
        total += other.astype(jnp.float32)
    return total


def scattered_sums(ins, ids, ready):
    top, bottom = part_sums(12, [4], ins, ids, ready)
    weights, top, bottom = lax.optimization_barrier((ins[0], top, bottom))
    ins = (weights,) + ins[1:]
    top, bottom = hop(top, 1, False), hop(bottom, -1, False)
    parts = part_sums(4, [3, 1, 3, 1], ins, ids)
    up_top, up_bottom, up_own_top, up_own_bottom, *parts = parts
    down_top, down_bottom, down_own_top, down_own_bottom = parts
    tops, bottoms = [hop(down_top, -1, False)], [hop(up_bottom, 1, False)]
    dtype = top.dtype
    up_top = added(up_top, [top[:3]]).astype(dtype)
    down_bottom = added(down_bottom, [bottom[:3]]).astype(dtype)
    weights, up_top, down_bottom = lax.optimization_barrier(
        (weights, up_top, down_bottom)
    )
    tops.append(hop(up_top, 1, False))
    bottoms.append(hop(down_bottom, -1, False))
    ins = (weights,) + ins[1:]
    near_top, near_bottom = part_sums(0, [4], ins, ids)
    up_own_top = added(up_own_top[0], [top[3]]).astype(dtype)
    down_own_bottom = added(down_own_bottom[0], [bottom[3]]).astype(dtype)
    last = [
        hop(jnp.concatenate([up_own_top, up_own_bottom[0]]), 1, False),
        hop(jnp.concatenate([down_own_top[0], down_own_bottom]), -1, False),
    ]
    for a, k in enumerate(OFFS):
        total = [
            added(near_top[a], [got[a] for got in tops]),
            added(near_bottom[a], [got[a] for got in bottoms]),
        ]
        last.append(hop(jnp.concatenate(total).astype(dtype), k, True))
    total = added(jnp.concatenate([near_top[3], near_bottom[3]]), last)
    rows = total.shape[0] - EXTRA
    half = rows // 2
    row_sums = total[half, :rows]
    means = jnp.concatenate([total[:half], total[half + EXTRA :]])
    return means / row_sums[:, None]


def body(noise_latents, data_latents):
    width = data_latents.shape[1]
    place = lax.axis_index("dp")
    core = place % 2
    z = (place // 2) % SIDE
    y = place // (2 * SIDE)
    ids = block_ids(y, z, core)
    data_other = swap(data_latents)
    held, _ = held_blocks(ids, 0, BLOCKS, data_latents, data_other)
    noise_f = noise_latents.astype(jnp.float32)
    sx_part = jnp.sum(noise_f * noise_f, axis=1)
    data_f = data_latents.astype(jnp.float32)
    sq_data = jnp.sum(data_f * data_f, axis=1)
    dots, sq_data = gathered_dots(noise_latents, held, sq_data)
    scale = 1.0 / (width * EPS)
    twice = dots * (2.0 * scale)
    sy = sq_data * scale
    sx = None
    g = jnp.zeros_like(sy)
    for step in range(ITERS):
        local = lse(twice + (g - sy)[None, :], 1)
        if sx is None:
            got = to_all_dp(jnp.stack([local, sx_part]))
            sx = jnp.sum(got[:, 1], axis=0) * scale
            got = got[:, 0]
        else:
            got = to_all_dp(local)
        f = sx - lse(got, 0)
        local = lse(twice + (f - sx)[:, None], 0)
        if step == ITERS - 1:
            local, ids = lax.optimization_barrier((local, ids))
        got = to_all_noise(local)
        if step == ITERS - 1:
            ready, mark = held_blocks(ids, 12, 4, data_latents, data_other)
            got, mark = lax.optimization_barrier((got, mark))
        g = sy - lse(got, 0)
    coupling = jnp.exp(twice + (f - sx)[:, None] + (g - sy)[None, :])
    weights = coupling.astype(jnp.bfloat16)
    means = scattered_sums(
        (weights, swap(weights), data_latents, data_other), ids, [ready, mark]
    )
    return means.astype(jnp.bfloat16)


def solution(mesh):
    return jax.shard_map(
        body,
        mesh=mesh,
        in_specs=(P("noise", "dp"), P("dp", None)),
        out_specs=P("noise", "dp"),
        check_vma=False,
    )
```

```python
import jax
import jax.numpy as jnp
from jax import lax
from jax.experimental import pallas as pl
from jax.experimental.pallas import tpu as pltpu
from jax.sharding import PartitionSpec as P

ITERS = 3
EPS = 0.004
SIDE = 4
OFFS = (2, 1, 3)
BLOCKS = SIDE * SIDE
EXTRA = 16
VMEM_LIMIT = 14 * 1024 * 1024

SPOTS = [(k, m) for k in (0, 1, 3, 2) for m in OFFS + (0,)]


def swap(values):
    n = lax.axis_size("dp")
    return lax.ppermute(values, "dp", [(i, i ^ 1) for i in range(n)])


def hop(values, k, first):
    pairs = []
    for y in range(SIDE):
        for z in range(SIDE):
            for c in range(2):
                along_z = (c == 0) == first
                to_y, to_z = (y, (z + k) % SIDE) if along_z else ((y + k) % SIDE, z)
                pairs.append(((y * SIDE + z) * 2 + c, (to_y * SIDE + to_z) * 2 + c))
    return lax.ppermute(values, "dp", pairs)


def block_ids(y, z, core):
    ids = []
    for k, m in SPOTS:
        dy = jnp.where(core == 0, k, m)
        dz = jnp.where(core == 0, m, k)
        ids.append((((y + dy) % SIDE) * SIDE + (z + dz) % SIDE) * 2 + core)
    return jnp.stack(ids).astype(jnp.int32)


def lse(values, axis):
    peak = jnp.max(values, axis=axis, keepdims=True)
    total = jnp.sum(jnp.exp(values - peak), axis=axis)
    return jnp.squeeze(peak, axis) + jnp.log(total)


def to_all_dp(values):
    n = lax.axis_size("dp")
    return lax.all_to_all(
        jnp.broadcast_to(values[None], (n,) + values.shape), "dp", 0, 0
    )


def to_all_noise(values):
    n = lax.axis_size("noise")
    parts = [values]
    for k in sorted(range(1, n), key=lambda k: -min(k, n - k)):
        parts.append(
            lax.ppermute(values, "noise", [(i, (i + k) % n) for i in range(n)])
        )
    return jnp.stack(parts)


def call(kernel, ins, in_specs, out_shape, out_specs, scratch, flops, moved):
    return pl.pallas_call(
        kernel,
        in_specs=in_specs,
        out_specs=out_specs,
        out_shape=out_shape,
        scratch_shapes=scratch,
        compiler_params=pltpu.CompilerParams(vmem_limit_bytes=VMEM_LIMIT),
        cost_estimate=pl.CostEstimate(
            flops=flops, bytes_accessed=moved, transcendentals=0
        ),
    )(*ins)


IN_SMEM = pl.BlockSpec(memory_space=pltpu.SMEM)
IN_VMEM = pl.BlockSpec(memory_space=pltpu.VMEM)
ANYWHERE = pl.BlockSpec(memory_space=pl.ANY)


def in_hbm(arrays):
    return [pltpu.with_memory_space_constraint(a, pltpu.HBM) for a in arrays]


def block_copies(ids_ref, t, refs, to, spot, sems):
    rows, width = refs[0].shape
    block = width // (2 * BLOCKS)
    place = pl.multiple_of(ids_ref[t] * block, block)
    return [
        pltpu.make_async_copy(
            ref.at[:, pl.ds(place, block)],
            to.at[pl.ds(b * rows, rows), pl.ds(spot * block, block)],
            sems.at[b, spot],
        )
        for b, ref in enumerate(refs)
    ]


def held_blocks(ids, start, n, data, data_other):
    rows, width = data.shape
    block = width // (2 * BLOCKS)

    def kernel(ids_ref, data_ref, data_other_ref, held, mark, sems):
        copies = []
        for t in range(n):
            copies += block_copies(
                ids_ref, start + t, (data_ref, data_other_ref), held, t, sems
            )
        for copy in copies:
            copy.start()
        mark[...] = jnp.zeros_like(mark)
        for copy in copies:
            copy.wait()

    return call(
        kernel,
        [ids] + in_hbm([data, data_other]),
        [IN_SMEM, ANYWHERE, ANYWHERE],
        [
            pltpu.VMEM((2 * rows, n * block), data.dtype),
            jax.ShapeDtypeStruct((8, 128), jnp.float32),
        ],
        [IN_VMEM, IN_VMEM],
        [pltpu.SemaphoreType.DMA((2, n))],
        0,
        n * rows * block * 8,
    )


def part_dots(start, groups, held, before, side=None):
    rows, block = groups[0].shape[1:]
    both = held.shape[0]
    mine = slice(0, both)
    if side is not None:
        mine = slice(side * both // 2, (side + 1) * both // 2)
    width = mine.stop - mine.start
    spots = [(a, i) for a, g in enumerate(groups) for i in range(g.shape[0])]

    def kernel(*refs):
        pieces, (held_ref, *rest) = refs[: len(groups)], refs[len(groups) :]
        total = None if before is None else rest[0][:, mine]
        for t, (a, i) in enumerate(spots):
            part = lax.dot_general(
                pieces[a][i],
                held_ref[mine, (start + t) * block : (start + t + 1) * block],
                (((1,), (1,)), ((), ())),
                preferred_element_type=jnp.float32,
            )
            total = part if total is None else total + part
        rest[-1][...] = total

    ins = groups + [held] + ([] if before is None else [before])
    return call(
        kernel,
        ins,
        [IN_VMEM] * len(ins),
        jax.ShapeDtypeStruct((rows, width), jnp.float32),
        IN_VMEM,
        [],
        len(spots) * 2 * rows * width * block,
        len(spots) * block * 2 * (width + rows),
    )


def gathered_dots(noise, held, sq_data):
    along = [hop(noise, -k, True) for k in OFFS] + [noise]
    one, two = jnp.stack(along[:2]), jnp.stack(along[2:])
    one, two, sq_data = lax.optimization_barrier((one, two, sq_data))
    up_one, down_two = hop(one, -1, False), hop(two, 1, False)
    up_two, down_one = hop(two, -1, False), hop(one, 1, False)
    dots = part_dots(0, [one, two], held, None)
    up_one, down_two, dots = lax.optimization_barrier((up_one, down_two, dots))
    far = [hop(up_one, -1, False), hop(down_two, 1, False)]
    dots = part_dots(4, [up_one, up_two, down_one, down_two], held, dots)
    other = swap(part_dots(12, far, held, dots, 1))
    return part_dots(12, far, held, dots, 0) + other, sq_data


def part_sums(start, groups, ins, ids, ready=None, step=2):
    w_own, w_oth, data, data_other = ins
    rows, inner = w_own.shape
    dtype = data.dtype
    block = data.shape[1] // (2 * BLOCKS)
    half = rows // 2
    ends = [sum(groups[: a + 1]) for a in range(len(groups))]
    count = ends[-1]
    sources = [data, data_other] if ready is None else ready

    def kernel(ids_ref, w_own_ref, w_oth_ref, *refs):
        refs, outs, scratch = (
            refs[: len(sources)],
            refs[len(sources) : len(sources) + 2 * len(groups)],
            refs[len(sources) + 2 * len(groups) :],
        )
        weights, tops, bottoms, sems, *scratch = scratch
        into = [[]] * count
        if ready is None:
            held, in_sems = scratch
            into = [
                block_copies(ids_ref, start + spot, refs, held, spot, in_sems)
                for spot in range(count)
            ]
            for copies in into:
                for copy in copies:
                    copy.start()
        else:
            held, _ = refs
        weights[:, :inner] = w_own_ref[...]
        weights[:, inner:] = w_oth_ref[...]
        ones = jnp.ones((EXTRA, 2 * inner), dtype)
        row_sums = lax.dot_general(
            ones,
            weights[...],
            (((1,), (1,)), ((), ())),
            preferred_element_type=jnp.float32,
        ).astype(dtype)
        for spot in range(count):
            tops[spot, half:, :rows] = row_sums
            tops[spot, half:, rows:] = jnp.zeros((EXTRA, block - rows), dtype)
        out = []
        for spot in range(0, count, step):
            stop = spot + step
            for copies in into[spot:stop]:
                for copy in copies:
                    copy.wait()
            total = jnp.dot(
                weights[...],
                held[:, spot * block : stop * block],
                preferred_element_type=jnp.float32,
            ).astype(dtype)
            for j in range(step):
                part = total[:, j * block : (j + 1) * block]
                tops[spot + j, :half] = part[:half]
                bottoms[spot + j] = part[half:]
            for a, n in enumerate(groups):
                if not spot < ends[a] <= stop:
                    continue
                for p, source in enumerate((tops, bottoms)):
                    to = 2 * a + p
                    out.append(
                        pltpu.make_async_copy(
                            source.at[pl.ds(ends[a] - n, n)], outs[to], sems.at[to]
                        )
                    )
                    out[-1].start()
        for copy in out:
            copy.wait()

    shapes = []
    for n in groups:
        shapes.append(jax.ShapeDtypeStruct((n, half + EXTRA, block), dtype))
        shapes.append(jax.ShapeDtypeStruct((n, half, block), dtype))
    scratch = [
        pltpu.VMEM((rows, 2 * inner), dtype),
        pltpu.VMEM((count, half + EXTRA, block), dtype),
        pltpu.VMEM((count, half, block), dtype),
        pltpu.SemaphoreType.DMA((2 * len(groups),)),
    ]
    if ready is None:
        scratch.append(pltpu.VMEM((2 * inner, count * block), dtype))
        scratch.append(pltpu.SemaphoreType.DMA((2, count)))
        sources = in_hbm(sources)
    return call(
        kernel,
        [ids, w_own, w_oth] + sources,
        [IN_SMEM, IN_VMEM, IN_VMEM]
        + [ANYWHERE if ready is None else IN_VMEM] * 2,
        shapes,
        [ANYWHERE] * len(shapes),
        scratch,
        count * 4 * rows * inner * block,
        count * 2 * block * (2 * inner + rows),
    )


def added(first, others):
    total = first.astype(jnp.float32)
    for other in others:
        total += other.astype(jnp.float32)
    return total


def scattered_sums(ins, ids, ready):
    top, bottom = part_sums(12, [4], ins, ids, ready)
    weights, top, bottom = lax.optimization_barrier((ins[0], top, bottom))
    ins = (weights,) + ins[1:]
    top, bottom = hop(top, 1, False), hop(bottom, -1, False)
    parts = part_sums(4, [3, 1, 3, 1], ins, ids)
    up_top, up_bottom, up_own_top, up_own_bottom, *parts = parts
    down_top, down_bottom, down_own_top, down_own_bottom = parts
    tops, bottoms = [hop(down_top, -1, False)], [hop(up_bottom, 1, False)]
    dtype = top.dtype
    up_top = added(up_top, [top[:3]]).astype(dtype)
    down_bottom = added(down_bottom, [bottom[:3]]).astype(dtype)
    weights, up_top, down_bottom = lax.optimization_barrier(
        (weights, up_top, down_bottom)
    )
    tops.append(hop(up_top, 1, False))
    bottoms.append(hop(down_bottom, -1, False))
    ins = (weights,) + ins[1:]
    near_top, near_bottom = part_sums(0, [4], ins, ids)
    up_own_top = added(up_own_top[0], [top[3]]).astype(dtype)
    down_own_bottom = added(down_own_bottom[0], [bottom[3]]).astype(dtype)
    last = [
        hop(jnp.concatenate([up_own_top, up_own_bottom[0]]), 1, False),
        hop(jnp.concatenate([down_own_top[0], down_own_bottom]), -1, False),
    ]
    for a, k in enumerate(OFFS):
        total = [
            added(near_top[a], [got[a] for got in tops]),
            added(near_bottom[a], [got[a] for got in bottoms]),
        ]
        last.append(hop(jnp.concatenate(total).astype(dtype), k, True))
    total = added(jnp.concatenate([near_top[3], near_bottom[3]]), last)
    rows = total.shape[0] - EXTRA
    half = rows // 2
    row_sums = total[half, :rows]
    means = jnp.concatenate([total[:half], total[half + EXTRA :]])
    return means / row_sums[:, None]


def body(noise_latents, data_latents):
    width = data_latents.shape[1]
    place = lax.axis_index("dp")
    core = place % 2
    z = (place // 2) % SIDE
    y = place // (2 * SIDE)
    ids = block_ids(y, z, core)
    data_other = swap(data_latents)
    held, _ = held_blocks(ids, 0, BLOCKS, data_latents, data_other)
    noise_f = noise_latents.astype(jnp.float32)
    sx_part = jnp.sum(noise_f * noise_f, axis=1)
    data_f = data_latents.astype(jnp.float32)
    sq_data = jnp.sum(data_f * data_f, axis=1)
    dots, sq_data = gathered_dots(noise_latents, held, sq_data)
    scale = 1.0 / (width * EPS)
    twice = dots * (2.0 * scale)
    sy = sq_data * scale
    sx = None
    g = jnp.zeros_like(sy)
    for step in range(ITERS):
        local = lse(twice + (g - sy)[None, :], 1)
        if sx is None:
            got = to_all_dp(jnp.stack([local, sx_part]))
            sx = jnp.sum(got[:, 1], axis=0) * scale
            got = got[:, 0]
        else:
            got = to_all_dp(local)
        f = sx - lse(got, 0)
        scores = twice + (f - sx)[:, None]
        if step == ITERS - 1:
            scores = lax.optimization_barrier(scores)
        local = lse(scores, 0)
        if step == ITERS - 1:
            local, ids = lax.optimization_barrier((local, ids))
        got = to_all_noise(local)
        if step == ITERS - 1:
            ready, mark = held_blocks(ids, 12, 4, data_latents, data_other)
            got, mark = lax.optimization_barrier((got, mark))
        g = sy - lse(got, 0)
    coupling = jnp.exp(scores + (g - sy)[None, :])
    weights = coupling.astype(jnp.bfloat16)
    means = scattered_sums(
        (weights, swap(weights), data_latents, data_other), ids, [ready, mark]
    )
    return means.astype(jnp.bfloat16)


def solution(mesh):
    return jax.shard_map(
        body,
        mesh=mesh,
        in_specs=(P("noise", "dp"), P("dp", None)),
        out_specs=P("noise", "dp"),
        check_vma=False,
    )
```
